768 devices in a mesh: gx: 6 (over z_hi, core), gy: 4 (over x), gz: 32 (over z_lo, y).
Axes of the slice: x: 4, y: 8, z: 12 (z_hi: 3, z_lo: 4; z = z_hi * 4 + z_lo), core: 2. Of those that a mesh axis runs over, the one named last changes fastest.
Arguments:
- orbitals: float32 [32, 192, 48, 96], P(None, 'gz', 'gx', 'gy'), may hold values from -6 to 6
- potential: float32 [192, 48, 96], P('gz', 'gx', 'gy'), may hold values from -2 to 0.5
- projectors: float32 [32, 6, 4, 64, 1152], P('gz', 'gx', 'gy'), may hold values from -0.1875 to 0.1875
- targets: int32 [32, 6, 4, 16], P('gz', 'gx', 'gy'), may hold values from 0 to 215
- coupling: float32 [32, 6, 4, 32], P('gz', 'gx', 'gy'), may hold values from 0.25 to 2
Outputs:
- filtered: float32 [32, 192, 48, 96], P(None, 'gz', 'gx', 'gy')
The draws below stay inside these ranges and needn't reach their ends.
Inputs may be any that keep to these rules, and one draw needn't show every extreme that they name: `targets`: A target g names atom g % 8 of the domain at offset (g // 72 - 1, g // 24 % 3 - 1, g // 8 % 3 - 1) in z, x, y from the slot's own domain, periodic; an atom may be named by several slots.
All inputs are finite; a program needn't handle non-finite values.
Results may differ from the reference program's by a relative error of at most 0.0001.
Values sent between devices are 32-bit elements; how exact they have to be, the bound alone decides.
A program may use at most 64 MiB of HBM per device.

```python
import math
import jax
import jax.numpy as jnp
from jax import lax

NORB = 32
NPJ = 4
DEGREE = 3
CZ = 6
CX = 8
CY = 24
ATOM_DEV = 8
SLOTS = 16
NZ = 192
NX = 48
NY = 96
CELLS = 1152
SEG = 216
PROWS = 64
N_GX = 6
N_GY = 4
N_GZ = 32


def place_ends(drawn, rng, least, largest):
    dims = drawn.shape
    spot = [jax.random.randint(jax.random.fold_in(rng, axis), (), 0, dims[axis]) for axis in range(len(dims))]
    drawn = drawn.at[tuple(spot)].set(least)
    longest = dims.index(max(dims))
    spot[longest] = (spot[longest] + 1) % dims[longest]
    return drawn.at[tuple(spot)].set(largest)


def steps_of(rng, extent, cuts, least, largest):
    def one(dim, parts):
        draws = jax.random.uniform(jax.random.fold_in(jax.random.fold_in(rng, 6), dim), (parts,), jnp.float32, least / len(cuts), largest / len(cuts))
        return jnp.repeat(jnp.exp(draws), extent[dim] // parts).reshape((-1,) + (1,) * (len(extent) - dim - 1))

    factor_of = one(*cuts[0])
    for cut in cuts[1:]:
        factor_of = factor_of * one(*cut)
    return factor_of


def normal_values(rng, shape, scale, limit, shards=(), kind=jnp.bfloat16):
    values = scale * jax.random.normal(rng, shape, jnp.float32)
    if shards:
        values = values * steps_of(rng, shape, shards, -0.22, 0.18)
    return jnp.clip(values, -limit, limit).astype(kind)


def setup_inputs(seed: int = 0) -> dict:
    streams_of = jax.random.split(jax.random.key(seed), 6)
    orbitals = normal_values(streams_of[0], (NORB, NZ, NX, NY), 1.0, 6.0, ((1, 32), (2, 6), (3, 4)), jnp.float32)
    potential = jnp.clip(-2.0 + 2.5 * jax.random.uniform(streams_of[1], (NZ, NX, NY), jnp.float32) ** steps_of(streams_of[1], (NZ, NX, NY), ((0, 32), (1, 6), (2, 4)), -0.2, 0.2), -2.0, 0.5)
    projectors = normal_values(streams_of[2], (N_GZ, N_GX, N_GY, PROWS, CELLS), CELLS ** -0.5, 0.1875, ((0, 32), (1, 6), (2, 4)), jnp.float32)
    targets = place_ends(jax.random.randint(streams_of[3], (N_GZ, N_GX, N_GY, SLOTS), 0, SEG), jax.random.fold_in(streams_of[3], 1), 0, SEG - 1).astype(jnp.int32)
    coupling = jnp.clip(jnp.exp(math.log(2.0) - 2.0794415 * jax.random.uniform(streams_of[4], (N_GZ, N_GX, N_GY, ATOM_DEV * NPJ), jnp.float32) ** steps_of(streams_of[4], (N_GZ, N_GX, N_GY, ATOM_DEV * NPJ), ((0, 32), (1, 6), (2, 4)), -0.2, 0.2)), 0.25, 2.0)
    return dict(orbitals=orbitals, potential=potential, projectors=projectors, targets=targets, coupling=coupling)


STENCIL = (-5369.0 / 1800.0, 12.0 / 7.0, -15.0 / 56.0, 10.0 / 189.0, -1.0 / 112.0, 2.0 / 1925.0, -1.0 / 16632.0)
LOWER_EDGE = 2.0
UPPER_EDGE = 16.0
HIGHEST = lax.Precision.HIGHEST


def laplacian(values_in):
    summed = (3.0 * STENCIL[0]) * values_in
    for dim_index in (1, 2, 3):
        for distance in range(1, 7):
            summed = summed + STENCIL[distance] * (jnp.roll(values_in, distance, dim_index) + jnp.roll(values_in, -distance, dim_index))
    return summed


def to_blocks(values_in):
    orbital_count = values_in.shape[0]
    shaped = values_in.reshape(orbital_count, N_GZ, CZ, N_GX, CX, N_GY, CY)
    return shaped.transpose(1, 3, 5, 0, 2, 4, 6).reshape(N_GZ, N_GX, N_GY, orbital_count, CZ * CX * CY)


def from_blocks(blocks):
    orbital_count = blocks.shape[3]
    shaped = blocks.reshape(N_GZ, N_GX, N_GY, orbital_count, CZ, CX, CY)
    return shaped.transpose(3, 0, 4, 1, 5, 2, 6).reshape(orbital_count, NZ, NX, NY)


def nonlocal_term(values_in, projectors, selector, coupling):
    blocks = to_blocks(values_in)
    partial_value = jnp.einsum("zxyrc,zxync->zxyrn", projectors, blocks, precision=HIGHEST)
    partial_value = partial_value.reshape(N_GZ, N_GX, N_GY, SLOTS, NPJ * NORB)
    grouped = jnp.einsum("zxygs,zxysk->zxygk", selector, partial_value, precision=HIGHEST)
    grouped = grouped.reshape(N_GZ, N_GX, N_GY, 27, ATOM_DEV * NPJ * NORB)
    summed = jnp.zeros((N_GZ, N_GX, N_GY, ATOM_DEV * NPJ * NORB), jnp.float32)
    for position in range(27):
        offsets = (position // 9 - 1, position // 3 % 3 - 1, position % 3 - 1)
        summed = summed + jnp.roll(grouped[:, :, :, position], offsets, (0, 1, 2))
    scaled = summed.reshape(N_GZ, N_GX, N_GY, ATOM_DEV * NPJ, NORB) * coupling[..., None]
    scaled = scaled.reshape(N_GZ, N_GX, N_GY, ATOM_DEV * NPJ * NORB)
    gathered = jnp.stack([jnp.roll(scaled, (1 - position // 9, 1 - position // 3 % 3, 1 - position % 3), (0, 1, 2)) for position in range(27)], axis=3)
    gathered = gathered.reshape(N_GZ, N_GX, N_GY, SEG, NPJ * NORB)
    picked = jnp.einsum("zxygs,zxygk->zxysk", selector, gathered, precision=HIGHEST)
    picked = picked.reshape(N_GZ, N_GX, N_GY, SLOTS * NPJ, NORB)
    returned = jnp.einsum("zxyrn,zxyrc->zxync", picked, projectors, precision=HIGHEST)
    return from_blocks(returned)


def reference(orbitals, potential, projectors, targets, coupling):
    selector = (jnp.arange(SEG, dtype=jnp.int32)[:, None] == targets[..., None, :]).astype(jnp.float32)
    centre = 0.5 * (UPPER_EDGE + LOWER_EDGE)
    spread = 0.5 * (UPPER_EDGE - LOWER_EDGE)

    def shifted(values_in):
        applied = -0.5 * laplacian(values_in) + potential[None] * values_in
        applied = applied + nonlocal_term(values_in, projectors, selector, coupling)
        return (applied - centre * values_in) / spread

    previous = orbitals
    current = shifted(orbitals)
    for degree_step in range(1, DEGREE):
        following = 2.0 * shifted(current) - previous
        previous, current = current, following
    return current
```

```python
import functools

import jax
import jax.numpy as jnp
from jax import lax
from jax.experimental import pallas as pl
from jax.experimental.pallas import tpu as pltpu
from jax.sharding import PartitionSpec as P

MESH = pl.DeviceIdType.MESH
F32, BF16 = jnp.float32, jnp.bfloat16

DEGREE = 3
NORB, NPJ, SLOTS, ATOM_DEV = 32, 4, 16, 8
CZ, CX, CY = 6, 8, 24
PROWS = SLOTS * NPJ
ZI, XI = CZ // 2, CX // 2
ROWS = ZI * XI * CY
SEG_CELLS = XI * CY

STENCIL = (
    -5369.0 / 1800.0,
    12.0 / 7.0,
    -15.0 / 56.0,
    10.0 / 189.0,
    -1.0 / 112.0,
    2.0 / 1925.0,
    -1.0 / 16632.0,
)
LOWER_EDGE = 2.0
UPPER_EDGE = 16.0
CENTRE = 0.5 * (UPPER_EDGE + LOWER_EDGE)
SPREAD = 0.5 * (UPPER_EDGE - LOWER_EDGE)
WEIGHT = tuple(-0.5 * c / SPREAD for c in STENCIL)

OFFSETS = [
    (a - 1, b - 1, c - 1)
    for a in range(3)
    for b in range(3)
    for c in range(3)
    if (a, b, c) != (1, 1, 1)
]
BESIDE = len(OFFSETS)


def split2(value):
    high = value.astype(BF16)
    low = (value - high.astype(F32)).astype(BF16)
    return high, low


def split3(value):
    high = value.astype(BF16)
    rest = value - high.astype(F32)
    mid = rest.astype(BF16)
    low = (rest - mid.astype(F32)).astype(BF16)
    return high, mid, low


def dot(a, b):
    return jnp.dot(a, b, preferred_element_type=F32)


def lanes_of(shape):
    return lax.broadcasted_iota(jnp.int32, shape, len(shape) - 1)


def roll(value, shift):
    return pltpu.roll(value, shift, value.ndim - 1)


def kernel(
    sizes,
    orb_hbm,
    pot_ref,
    proj_hbm,
    targets_ref,
    coupling_ref,
    out_ref,
    orb,
    proj,
    field,
    z_low,
    z_high,
    x_low,
    x_high,
    x_low_part,
    x_high_part,
    send_low_part,
    send_high_part,
    grouped,
    partials,
    scaled,
    gathered,
    rows_t,
    rows_hi,
    rows_lo,
    columns,
    choose,
    pick,
    factor,
    diagonal,
    pot_pad,
    local,
    in_sems,
    halo_send,
    halo_recv,
    sum_send,
    sum_recv,
    spread_send,
    spread_recv,
):
    me = {name: lax.axis_index(name) for name in ("gz", "gx", "gy")}

    def beside(offset):
        place = {
            name: lax.rem(me[name] + step + sizes[name], sizes[name])
            for name, step in zip(("gz", "gx", "gy"), offset)
        }
        return (place["gx"], place["gy"], place["gz"])

    targets = [beside(offset) for offset in OFFSETS]

    load_orb = pltpu.make_async_copy(orb_hbm, orb, in_sems.at[0])
    load_proj = pltpu.make_async_copy(proj_hbm, proj, in_sems.at[1])
    load_orb.start()
    load_proj.start()

    barrier = pltpu.get_barrier_semaphore()
    for place in targets:
        pl.semaphore_signal(barrier, inc=1, device_id=place, device_id_type=MESH)

    load_orb.wait()
    for zi in range(ZI):
        for xi in range(XI):
            for q in range(4):
                zb, xb = q // 2, q % 2
                field[0, zi, xi, 8:32, 32 * q : 32 * q + 32] = orb[zb * ZI + zi, xb * XI + xi]

    load_proj.wait()
    for q in range(4):
        zb, xb = q // 2, q % 2
        for zi in range(ZI):
            start = (zb * ZI + zi) * CX * CY + xb * SEG_CELLS
            rows_t[PROWS * q : PROWS * (q + 1), SEG_CELLS * zi : SEG_CELLS * (zi + 1)] = proj[
                :, start : start + SEG_CELLS
            ]
    rows_t[:, ROWS:384] = jnp.zeros((4 * PROWS, 384 - ROWS), F32)
    high, low = split2(rows_t[...])
    rows_hi[...] = high
    rows_lo[...] = low

    lane_slot = lanes_of((8, 256)) % PROWS // NPJ
    row_slot = lax.broadcasted_iota(jnp.int32, (PROWS, 256), 0) // NPJ
    named_lane = jnp.zeros((8, 256), jnp.int32)
    named_row = jnp.zeros((PROWS, 256), jnp.int32)
    own_first = ATOM_DEV * (BESIDE // 2)
    for s in range(SLOTS):
        atom = targets_ref[s]
        atom = jnp.where(
            atom < own_first,
            atom,
            jnp.where(atom < own_first + ATOM_DEV, atom + own_first, atom - ATOM_DEV),
        )
        named_lane = jnp.where(lane_slot == s, atom, named_lane)
        named_row = jnp.where(row_slot == s, atom, named_row)
    atom_row = lax.broadcasted_iota(jnp.int32, (8, 256), 0)
    used = lanes_of((8, 256)) < 3 * PROWS
    for j in range(BESIDE + 1):
        choose[8 * j : 8 * j + 8, :] = jnp.where(
            (named_lane == atom_row + 8 * j) & used, 1.0, 0.0
        )
    pick[...] = jnp.where(named_row == lanes_of((PROWS, 256)), 1.0, 0.0)
    pair = NPJ * lax.broadcasted_iota(jnp.int32, (8, 128), 0) + lanes_of((8, 128)) // NORB
    weights = jnp.zeros((8, 128), F32)
    for j in range(ATOM_DEV * NPJ):
        weights = jnp.where(pair == j, coupling_ref[j], weights)
    factor[...] = weights * (1.0 / SPREAD)

    group = lanes_of((PROWS, 128)) // NORB
    own_group = group == lax.broadcasted_iota(jnp.int32, (PROWS, 128), 0) % NPJ
    is_x1 = lanes_of((CY, 128)) % 64 >= 32
    is_z1 = lanes_of((CY, 128)) >= 64

    pl.semaphore_wait(barrier, BESIDE)

    def everywhere(masked):
        paired = masked + roll(masked, 64)
        return paired + roll(paired, 32)

    def send_sums(k):
        flat = field[k, :, :, 8:32, :].reshape(ROWS, 128)
        f_hi, f_lo = split2(flat)
        p_hi, p_lo = rows_hi[:, :ROWS], rows_lo[:, :ROWS]
        crossed = dot(p_hi, f_hi) + (dot(p_lo, f_hi) + dot(p_hi, f_lo))
        kept = crossed[3 * PROWS :]
        for q in range(3):
            kept = jnp.where(group == q, crossed[PROWS * q : PROWS * (q + 1)], kept)
        by_slot = jnp.where(own_group, everywhere(kept), 0.0)
        parts = split3(by_slot)
        stacked = jnp.concatenate(parts + (jnp.zeros((PROWS, 128), BF16),), axis=0)
        sums = dot(choose[...].astype(BF16), stacked)
        grouped[k] = sums.reshape(BESIDE + 1, 8, 128)
        copies = []
        for j, place in enumerate(targets):
            copies.append(
                pltpu.make_async_remote_copy(
                    src_ref=grouped.at[k, j],
                    dst_ref=partials.at[k, j],
                    send_sem=sum_send.at[k],
                    recv_sem=sum_recv.at[k],
                    device_id=place,
                    device_id_type=MESH,
                )
            )
            copies[-1].start()

    def halo_copies(k):
        own = field.at[k, :, :, pl.ds(8, CY), :]
        moves = (
            (field.at[k, :, pl.ds(2, 2), pl.ds(8, CY), :], x_low.at[k], (0, 1, 0)),
            (field.at[k, :, pl.ds(0, 2), pl.ds(8, CY), :], x_high.at[k], (0, -1, 0)),
            (send_low_part.at[k], x_low_part.at[k], (0, 1, 0)),
            (send_high_part.at[k], x_high_part.at[k], (0, -1, 0)),
            (own, z_low.at[k], (1, 0, 0)),
            (own, z_high.at[k], (-1, 0, 0)),
            (field.at[k, :, :, pl.ds(24, 8), :], field.at[k, :, :, pl.ds(0, 8), :], (0, 0, 1)),
            (field.at[k, :, :, pl.ds(8, 8), :], field.at[k, :, :, pl.ds(32, 8), :], (0, 0, -1)),
        )
        return [
            pltpu.make_async_remote_copy(
                src_ref=source,
                dst_ref=target,
                send_sem=halo_send.at[k, i],
                recv_sem=halo_recv.at[k, i],
                device_id=beside(offset),
                device_id_type=MESH,
            )
            for i, (source, target, offset) in enumerate(moves)
        ]

    def send_halos(k):
        for zi in range(ZI):
            cell = [field[k, zi, xi, 8:32, :] for xi in range(XI)]
            send_low_part[k, zi] = jnp.where(is_x1, cell[1], roll(cell[0], 96))
            send_high_part[k, zi] = jnp.where(is_x1, roll(cell[2], 32), cell[3])
        copies = halo_copies(k)
        for copy in copies:
            copy.start()
        return copies

    pot_pad[...] = jnp.zeros((128, 128), F32)
    pot_pad[: CZ * CX, :CY] = pot_ref[...]
    pot_t = pot_pad[...].T[:CY]
    pieces = split3(pot_t)
    stacked_pot = jnp.concatenate([p.astype(F32) for p in pieces], axis=0).astype(BF16)
    plane = lax.broadcasted_iota(jnp.int32, (128, 128), 0)
    lane = lanes_of((128, 128))
    wanted = (lane // 64 * ZI) * CX + lane // 32 % 2 * XI

    def fill_diagonal():
        for zi in range(ZI):
            for xi in range(XI):
                hot = jnp.where(plane == wanted + (zi * CX + xi), 1.0, 0.0).astype(BF16)
                got = dot(stacked_pot, hot)
                value = got[:CY] + (got[CY : 2 * CY] + got[2 * CY :])
                diagonal[zi, xi] = (value - (CENTRE + 1.5 * STENCIL[0])) * (1.0 / SPREAD)

    def fill_columns():
        transposed = rows_t[...].T[:ROWS]
        t_hi, t_lo = split2(transposed)
        columns[:, 0:256] = t_hi
        columns[:, 256:512] = t_lo
        columns[:, 512:768] = t_hi

    def send_atoms(k):
        pltpu.make_async_copy(partials.at[k], partials.at[k], sum_recv.at[k]).wait()
        total = grouped[k, BESIDE]
        for j in range(BESIDE):
            total = total + partials[k, j]
        total = total * factor[...]
        scaled[k] = total
        gathered[k, BESIDE] = total
        for j in range(BESIDE + 1, 32):
            gathered[k, j] = jnp.zeros((8, 128), F32)
        for j, place in enumerate(targets):
            pltpu.make_async_remote_copy(
                src_ref=scaled.at[k],
                dst_ref=gathered.at[k, BESIDE - 1 - j],
                send_sem=spread_send.at[k],
                recv_sem=spread_recv.at[k],
                device_id=place,
                device_id_type=MESH,
            ).start()

    def stencil(k, copies):
        for copy in copies:
            copy.wait_recv()
        for xi in range(XI):
            own = [field[k, zi, xi, 8:32, :] for zi in range(ZI)]
            low = [z_low[k, zi, xi] for zi in range(ZI)]
            high = [z_high[k, zi, xi] for zi in range(ZI)]
            before = [roll(jnp.where(is_z1, l, o), 64) for o, l in zip(own, low)]
            after = [roll(jnp.where(is_z1, o, h), 64) for o, h in zip(own, high)]
            line = low + before + own + after + high
            for zi in range(ZI):
                at = zi + 2 * ZI
                total = diagonal[zi, xi] * own[zi]
                for d in range(1, 7):
                    total = total + WEIGHT[d] * (line[at - d] + line[at + d])
                for d in range(1, 7):
                    total = total + WEIGHT[d] * (
                        field[k, zi, xi, 8 - d : 32 - d, :] + field[k, zi, xi, 8 + d : 32 + d, :]
                    )
                local[zi, xi] = total
        for zi in range(ZI):
            own = [field[k, zi, xi, 8:32, :] for xi in range(XI)]
            up = [roll(o, 32) for o in own]
            down = [roll(o, 96) for o in own]
            low = [x_low[k, zi, i] for i in range(2)]
            high = [x_high[k, zi, i] for i in range(2)]
            low_part, high_part = x_low_part[k, zi], x_high_part[k, zi]
            before = [
                jnp.where(is_x1, up[0], low_part),
                jnp.where(is_x1, up[1], roll(low_part, 96)),
                jnp.where(is_x1, up[2], roll(low[0], 96)),
                jnp.where(is_x1, up[3], roll(low[1], 96)),
            ]
            after = [
                jnp.where(is_x1, roll(high[0], 32), down[0]),
                jnp.where(is_x1, roll(high[1], 32), down[1]),
                jnp.where(is_x1, high_part, down[2]),
                jnp.where(is_x1, roll(high_part, 32), down[3]),
            ]
            line = low + before + own + after + high
            for xi in range(XI):
                at = xi + 6
                total = local[zi, xi]
                for d in range(1, 7):
                    total = total + WEIGHT[d] * (line[at - d] + line[at + d])
                local[zi, xi] = total

    def nonlocal_part(k):
        landed = gathered.at[k, pl.ds(0, BESIDE)]
        pltpu.make_async_copy(landed, landed, spread_recv.at[k]).wait()
        around = gathered[k].reshape(256, 128)
        hot = pick[...].astype(BF16)
        a, b, c = split3(around)
        picked = dot(hot, a) + (dot(hot, b) + dot(hot, c))
        rep = everywhere(jnp.where(own_group, picked, 0.0))
        blocks = jnp.concatenate([jnp.where(group == q, rep, 0.0) for q in range(4)], axis=0)
        b_hi, b_lo = split2(blocks)
        return dot(columns[...], jnp.concatenate([b_hi, b_hi, b_lo], axis=0))

    started = []
    for k in range(DEGREE):
        send_sums(k)
        copies = send_halos(k)
        started += copies
        if k == 0:
            fill_diagonal()
            fill_columns()
        send_atoms(k)
        stencil(k, copies)
        returned = nonlocal_part(k).reshape(ZI, XI, CY, 128)
        for zi in range(ZI):
            for xi in range(XI):
                value = local[zi, xi] + returned[zi, xi]
                if k > 0:
                    value = 2.0 * value - field[k - 1, zi, xi, 8:32, :]
                if k < DEGREE - 1:
                    field[k + 1, zi, xi, 8:32, :] = value
                else:
                    for q in range(4):
                        zb, xb = q // 2, q % 2
                        out_ref[zb * ZI + zi, xb * XI + xi] = value[:, 32 * q : 32 * q + 32]

    for copy in started:
        copy.wait_send()
    for k in range(DEGREE):
        sent = grouped.at[k, pl.ds(0, BESIDE)]
        pltpu.make_async_copy(sent, sent, sum_send.at[k]).wait()
        pltpu.make_async_copy(sent, sent, spread_send.at[k]).wait()


def shards(sizes, orbitals, potential, projectors, targets, coupling):
    cells = orbitals.transpose(1, 2, 3, 0)
    any_space = pl.BlockSpec(memory_space=pl.ANY)
    vmem = pl.BlockSpec(memory_space=pltpu.VMEM)
    smem = pl.BlockSpec(memory_space=pltpu.SMEM)
    steps = DEGREE
    result = pl.pallas_call(
        functools.partial(kernel, sizes),
        out_shape=jax.ShapeDtypeStruct((CZ, CX, CY, NORB), F32),
        in_specs=[any_space, vmem, any_space, smem, smem],
        out_specs=vmem,
        scratch_shapes=[
            pltpu.VMEM((CZ, CX, CY, NORB), F32),
            pltpu.VMEM((PROWS, CZ * CX * CY), F32),
            pltpu.VMEM((steps, ZI, XI, CY + 16, 128), F32),
            pltpu.VMEM((steps, ZI, XI, CY, 128), F32),
            pltpu.VMEM((steps, ZI, XI, CY, 128), F32),
            pltpu.VMEM((steps, ZI, 2, CY, 128), F32),
            pltpu.VMEM((steps, ZI, 2, CY, 128), F32),
            pltpu.VMEM((steps, ZI, CY, 128), F32),
            pltpu.VMEM((steps, ZI, CY, 128), F32),
            pltpu.VMEM((steps, ZI, CY, 128), F32),
            pltpu.VMEM((steps, ZI, CY, 128), F32),
            pltpu.VMEM((steps, BESIDE + 1, 8, 128), F32),
            pltpu.VMEM((steps, BESIDE, 8, 128), F32),
            pltpu.VMEM((steps, 8, 128), F32),
            pltpu.VMEM((steps, 32, 8, 128), F32),
            pltpu.VMEM((4 * PROWS, 384), F32),
            pltpu.VMEM((4 * PROWS, 384), BF16),
            pltpu.VMEM((4 * PROWS, 384), BF16),
            pltpu.VMEM((ROWS, 768), BF16),
            pltpu.VMEM((8 * (BESIDE + 1), 256), F32),
            pltpu.VMEM((PROWS, 256), F32),
            pltpu.VMEM((8, 128), F32),
            pltpu.VMEM((ZI, XI, CY, 128), F32),
            pltpu.VMEM((128, 128), F32),
            pltpu.VMEM((ZI, XI, CY, 128), F32),
            pltpu.SemaphoreType.DMA((2,)),
            pltpu.SemaphoreType.DMA((steps, 8)),
            pltpu.SemaphoreType.DMA((steps, 8)),
            pltpu.SemaphoreType.DMA((steps,)),
            pltpu.SemaphoreType.DMA((steps,)),
            pltpu.SemaphoreType.DMA((steps,)),
            pltpu.SemaphoreType.DMA((steps,)),
        ],
        compiler_params=pltpu.CompilerParams(
            collective_id=0, has_side_effects=True, vmem_limit_bytes=40 * 1024 * 1024
        ),
    )(
        cells,
        potential.reshape(CZ * CX, CY),
        projectors.reshape(PROWS, CZ * CX * CY),
        targets.reshape(SLOTS),
        coupling.reshape(ATOM_DEV * NPJ),
    )
    return result.transpose(3, 0, 1, 2)


def solution(mesh):
    sizes = {name: mesh.shape[name] for name in ("gx", "gy", "gz")}
    return jax.shard_map(
        functools.partial(shards, sizes),
        mesh=mesh,
        in_specs=(
            P(None, "gz", "gx", "gy"),
            P("gz", "gx", "gy"),
            P("gz", "gx", "gy", None, None),
            P("gz", "gx", "gy", None),
            P("gz", "gx", "gy", None),
        ),
        out_specs=P(None, "gz", "gx", "gy"),
        check_vma=False,
    )
```

```python
import functools

import jax
import jax.numpy as jnp
from jax import lax
from jax.experimental import pallas as pl
from jax.experimental.pallas import tpu as pltpu
from jax.sharding import PartitionSpec as P

MESH = pl.DeviceIdType.MESH
F32, BF16 = jnp.float32, jnp.bfloat16

DEGREE = 3
NORB, NPJ, SLOTS, ATOM_DEV = 32, 4, 16, 8
CZ, CX, CY = 6, 8, 24
PROWS = SLOTS * NPJ
ZI, XI = CZ // 2, CX // 2
ROWS = ZI * XI * CY
SEG_CELLS = XI * CY

STENCIL = (
    -5369.0 / 1800.0,
    12.0 / 7.0,
    -15.0 / 56.0,
    10.0 / 189.0,
    -1.0 / 112.0,
    2.0 / 1925.0,
    -1.0 / 16632.0,
)
LOWER_EDGE = 2.0
UPPER_EDGE = 16.0
CENTRE = 0.5 * (UPPER_EDGE + LOWER_EDGE)
SPREAD = 0.5 * (UPPER_EDGE - LOWER_EDGE)
WEIGHT = tuple(-0.5 * c / SPREAD for c in STENCIL)

OFFSETS = [
    (a - 1, b - 1, c - 1)
    for a in range(3)
    for b in range(3)
    for c in range(3)
    if (a, b, c) != (1, 1, 1)
]
BESIDE = len(OFFSETS)


def split2(value):
    high = value.astype(BF16)
    low = (value - high.astype(F32)).astype(BF16)
    return high, low


def split3(value):
    high = value.astype(BF16)
    rest = value - high.astype(F32)
    mid = rest.astype(BF16)
    low = (rest - mid.astype(F32)).astype(BF16)
    return high, mid, low


def dot(a, b):
    return jnp.dot(a, b, preferred_element_type=F32)


def lanes_of(shape):
    return lax.broadcasted_iota(jnp.int32, shape, len(shape) - 1)


def roll(value, shift):
    return pltpu.roll(value, shift, value.ndim - 1)


def kernel(
    sizes,
    orb_hbm,
    pot_hbm,
    proj_hbm,
    targets_hbm,
    coupling_hbm,
    out_ref,
    orb,
    proj,
    pot_ref,
    targets_ref,
    coupling_ref,
    field,
    z_low,
    z_high,
    x_low,
    x_high,
    x_low_part,
    x_high_part,
    send_low_part,
    send_high_part,
    grouped,
    partials,
    scaled,
    gathered,
    rows_t,
    rows_hi,
    rows_lo,
    columns,
    choose,
    pick,
    overlap,
    factor,
    diagonal,
    pot_pad,
    local,
    in_sems,
    halo_send,
    halo_recv,
    sum_send,
    sum_recv,
    spread_send,
    spread_recv,
):
    me = {name: lax.axis_index(name) for name in ("gz", "gx", "gy")}

    def beside(offset):
        place = {
            name: lax.rem(me[name] + step + sizes[name], sizes[name])
            for name, step in zip(("gz", "gx", "gy"), offset)
        }
        return (place["gx"], place["gy"], place["gz"])

    targets = [beside(offset) for offset in OFFSETS]

    barrier = pltpu.get_barrier_semaphore()
    for place in targets:
        pl.semaphore_signal(barrier, inc=1, device_id=place, device_id_type=MESH)

    loads = [
        pltpu.make_async_copy(source, target, in_sems.at[i])
        for i, (source, target) in enumerate(
            (
                (orb_hbm, orb),
                (proj_hbm, proj),
                (targets_hbm, targets_ref),
                (coupling_hbm, coupling_ref),
                (pot_hbm, pot_ref),
            )
        )
    ]
    for load in loads:
        load.start()

    loads[0].wait()
    for zi in range(ZI):
        for xi in range(XI):
            for q in range(4):
                zb, xb = q // 2, q % 2
                field[0, zi, xi, 8:32, 32 * q : 32 * q + 32] = orb[zb * ZI + zi, xb * XI + xi]

    loads[1].wait()
    for q in range(4):
        zb, xb = q // 2, q % 2
        for zi in range(ZI):
            start = (zb * ZI + zi) * CX * CY + xb * SEG_CELLS
            rows_t[PROWS * q : PROWS * (q + 1), SEG_CELLS * zi : SEG_CELLS * (zi + 1)] = proj[
                :, start : start + SEG_CELLS
            ]
    rows_t[:, ROWS:384] = jnp.zeros((4 * PROWS, 384 - ROWS), F32)
    high, low = split2(rows_t[...])
    rows_hi[...] = high
    rows_lo[...] = low

    loads[2].wait()
    loads[3].wait()
    lane_slot = lanes_of((8, 128)) % PROWS // NPJ
    row_slot = lax.broadcasted_iota(jnp.int32, (PROWS, 256), 0) // NPJ
    named_lane = jnp.zeros((8, 128), jnp.int32)
    named_row = jnp.zeros((PROWS, 256), jnp.int32)
    own_first = ATOM_DEV * (BESIDE // 2)
    for s in range(SLOTS):
        atom = targets_ref[s]
        atom = jnp.where(
            atom < own_first,
            atom,
            jnp.where(atom < own_first + ATOM_DEV, atom + own_first, atom - ATOM_DEV),
        )
        named_lane = jnp.where(lane_slot == s, atom, named_lane)
        named_row = jnp.where(row_slot == s, atom, named_row)
    atom_row = lax.broadcasted_iota(jnp.int32, (8, 128), 0)
    for j in range(BESIDE + 1):
        choose[8 * j : 8 * j + 8, :] = jnp.where(named_lane == atom_row + 8 * j, 1.0, 0.0)
    pick[...] = jnp.where(named_row == lanes_of((PROWS, 256)), 1.0, 0.0).astype(BF16)
    for k in range(DEGREE):
        for j in range(BESIDE + 1, 32):
            gathered[k, j] = jnp.zeros((8, 128), F32)
    pair = NPJ * lax.broadcasted_iota(jnp.int32, (8, 128), 0) + lanes_of((8, 128)) // NORB
    weights = jnp.zeros((8, 128), F32)
    for j in range(ATOM_DEV * NPJ):
        weights = jnp.where(pair == j, coupling_ref[j], weights)
    factor[...] = weights * (1.0 / SPREAD)

    group = lanes_of((PROWS, 128)) // NORB
    own_group = group == lax.broadcasted_iota(jnp.int32, (PROWS, 128), 0) % NPJ
    is_x1 = lanes_of((CY, 128)) % 64 >= 32
    is_z1 = lanes_of((CY, 128)) >= 64

    def everywhere(masked):
        paired = masked + roll(masked, 64)
        return paired + roll(paired, 32)

    def products(cells):
        f_hi, f_lo = split2(cells.reshape(ROWS, 128))
        p_hi, p_lo = rows_hi[:, :ROWS], rows_lo[:, :ROWS]
        crossed = dot(p_hi, f_hi) + (dot(p_lo, f_hi) + dot(p_hi, f_lo))
        kept = crossed[3 * PROWS :]
        for q in range(3):
            kept = jnp.where(group == q, crossed[PROWS * q : PROWS * (q + 1)], kept)
        return everywhere(kept)

    def group_sums(k, by_row):
        stacked = jnp.concatenate(split2(jnp.where(own_group, by_row, 0.0)), axis=0)
        grouped[k] = dot(choose[...].astype(BF16), stacked).reshape(BESIDE + 1, 8, 128)

    def send_sums(k):
        for j, place in enumerate(targets):
            pltpu.make_async_remote_copy(
                src_ref=grouped.at[k, j],
                dst_ref=partials.at[k, j],
                send_sem=sum_send.at[k],
                recv_sem=sum_recv.at[k],
                device_id=place,
                device_id_type=MESH,
            ).start()

    def halo_copies(k):
        own = field.at[k, :, :, pl.ds(8, CY), :]
        moves = (
            (field.at[k, :, pl.ds(2, 2), pl.ds(8, CY), :], x_low.at[k], (0, 1, 0)),
            (field.at[k, :, pl.ds(0, 2), pl.ds(8, CY), :], x_high.at[k], (0, -1, 0)),
            (send_low_part.at[k], x_low_part.at[k], (0, 1, 0)),
            (send_high_part.at[k], x_high_part.at[k], (0, -1, 0)),
            (own, z_low.at[k], (1, 0, 0)),
            (own, z_high.at[k], (-1, 0, 0)),
            (field.at[k, :, :, pl.ds(24, 8), :], field.at[k, :, :, pl.ds(0, 8), :], (0, 0, 1)),
            (field.at[k, :, :, pl.ds(8, 8), :], field.at[k, :, :, pl.ds(32, 8), :], (0, 0, -1)),
        )
        return [
            pltpu.make_async_remote_copy(
                src_ref=source,
                dst_ref=target,
                send_sem=halo_send.at[k, i],
                recv_sem=halo_recv.at[k, i],
                device_id=beside(offset),
                device_id_type=MESH,
            )
            for i, (source, target, offset) in enumerate(moves)
        ]

    def send_halos(k):
        for zi in range(ZI):
            cell = [field[k, zi, xi, 8:32, :] for xi in range(XI)]
            send_low_part[k, zi] = jnp.where(is_x1, cell[1], roll(cell[0], 96))
            send_high_part[k, zi] = jnp.where(is_x1, roll(cell[2], 32), cell[3])
        copies = halo_copies(k)
        for copy in copies:
            copy.start()
        return copies

    def fill_overlap():
        o_hi, o_lo = split2(proj[...])

        def rows_by_rows(a, b):
            return lax.dot_general(a, b, (((1,), (1,)), ((), ())), preferred_element_type=F32)

        gram = rows_by_rows(o_hi, o_hi) + (rows_by_rows(o_hi, o_lo) + rows_by_rows(o_lo, o_hi))
        g_hi, g_lo = split2(gram)
        overlap[0] = g_hi
        overlap[1] = g_lo

    loads[4].wait()
    pot_pad[...] = jnp.zeros((128, 128), F32)
    pot_pad[: CZ * CX, :CY] = pot_ref[...]
    pot_t = pot_pad[...].T[:CY]
    pieces = split3(pot_t)
    stacked_pot = jnp.concatenate([p.astype(F32) for p in pieces], axis=0).astype(BF16)
    plane = lax.broadcasted_iota(jnp.int32, (128, 128), 0)
    lane = lanes_of((128, 128))
    wanted = (lane // 64 * ZI) * CX + lane // 32 % 2 * XI

    def fill_diagonal():
        for zi in range(ZI):
            for xi in range(XI):
                hot = jnp.where(plane == wanted + (zi * CX + xi), 1.0, 0.0).astype(BF16)
                got = dot(stacked_pot, hot)
                value = got[:CY] + (got[CY : 2 * CY] + got[2 * CY :])
                diagonal[zi, xi] = (value - (CENTRE + 1.5 * STENCIL[0])) * (1.0 / SPREAD)

    def fill_columns():
        transposed = rows_t[...].T[:ROWS]
        t_hi, t_lo = split2(transposed)
        columns[:, 0:256] = t_hi
        columns[:, 256:512] = t_lo
        columns[:, 512:768] = t_hi

    def send_atoms(k):
        pltpu.make_async_copy(partials.at[k], partials.at[k], sum_recv.at[k]).wait()
        total = grouped[k, BESIDE]
        for j in range(BESIDE):
            total = total + partials[k, j]
        total = total * factor[...]
        scaled[k] = total
        gathered[k, BESIDE] = total
        for j, place in enumerate(targets):
            pltpu.make_async_remote_copy(
                src_ref=scaled.at[k],
                dst_ref=gathered.at[k, BESIDE - 1 - j],
                send_sem=spread_send.at[k],
                recv_sem=spread_recv.at[k],
                device_id=place,
                device_id_type=MESH,
            ).start()

    def stencil(k, copies):
        for copy in copies:
            copy.wait_recv()
        for xi in range(XI):
            own = [field[k, zi, xi, 8:32, :] for zi in range(ZI)]
            low = [z_low[k, zi, xi] for zi in range(ZI)]
            high = [z_high[k, zi, xi] for zi in range(ZI)]
            before = [roll(jnp.where(is_z1, l, o), 64) for o, l in zip(own, low)]
            after = [roll(jnp.where(is_z1, o, h), 64) for o, h in zip(own, high)]
            line = low + before + own + after + high
            for zi in range(ZI):
                at = zi + 2 * ZI
                total = diagonal[zi, xi] * own[zi]
                for d in range(1, 7):
                    total = total + WEIGHT[d] * (line[at - d] + line[at + d])
                for d in range(1, 7):
                    total = total + WEIGHT[d] * (
                        field[k, zi, xi, 8 - d : 32 - d, :] + field[k, zi, xi, 8 + d : 32 + d, :]
                    )
                local[zi, xi] = total
        for zi in range(ZI):
            own = [field[k, zi, xi, 8:32, :] for xi in range(XI)]
            up = [roll(o, 32) for o in own]
            down = [roll(o, 96) for o in own]
            low = [x_low[k, zi, i] for i in range(2)]
            high = [x_high[k, zi, i] for i in range(2)]
            low_part, high_part = x_low_part[k, zi], x_high_part[k, zi]
            before = [
                jnp.where(is_x1, up[0], low_part),
                jnp.where(is_x1, up[1], roll(low_part, 96)),
                jnp.where(is_x1, up[2], roll(low[0], 96)),
                jnp.where(is_x1, up[3], roll(low[1], 96)),
            ]
            after = [
                jnp.where(is_x1, roll(high[0], 32), down[0]),
                jnp.where(is_x1, roll(high[1], 32), down[1]),
                jnp.where(is_x1, high_part, down[2]),
                jnp.where(is_x1, roll(high_part, 32), down[3]),
            ]
            line = low + before + own + after + high
            for xi in range(XI):
                at = xi + 6
                total = local[zi, xi]
                for d in range(1, 7):
                    total = total + WEIGHT[d] * (line[at - d] + line[at + d])
                local[zi, xi] = total

    def scale_local(k):
        if k > 0:
            for zi in range(ZI):
                for xi in range(XI):
                    local[zi, xi] = 2.0 * local[zi, xi] - field[k - 1, zi, xi, 8:32, :]

    def picked_rows(k):
        landed = gathered.at[k, pl.ds(0, BESIDE)]
        pltpu.make_async_copy(landed, landed, spread_recv.at[k]).wait()
        a, b = split2(gathered[k].reshape(256, 128))
        hot = pick[...]
        picked = dot(hot, a) + dot(hot, b)
        rep = everywhere(jnp.where(own_group, picked, 0.0))
        return rep if k == 0 else 2.0 * rep

    def projected(rep):
        r_hi, r_lo = split2(rep)
        return dot(overlap[0], r_hi) + (dot(overlap[1], r_hi) + dot(overlap[0], r_lo))

    def nonlocal_part(rep):
        blocks = jnp.concatenate([jnp.where(group == q, rep, 0.0) for q in range(4)], axis=0)
        b_hi, b_lo = split2(blocks)
        return dot(columns[...], jnp.concatenate([b_hi, b_hi, b_lo], axis=0))

    group_sums(0, products(field[0, :, :, 8:32, :]))
    pl.semaphore_wait(barrier, BESIDE)
    send_sums(0)
    copies = send_halos(0)
    started = list(copies)
    fill_diagonal()
    fill_columns()
    fill_overlap()
    for k in range(DEGREE):
        send_atoms(k)
        stencil(k, copies)
        scale_local(k)
        if k < DEGREE - 1:
            ready = products(local[...])
        rep = picked_rows(k)
        if k < DEGREE - 1:
            group_sums(k + 1, ready + projected(rep))
            send_sums(k + 1)
        returned = nonlocal_part(rep).reshape(ZI, XI, CY, 128)
        for zi in range(ZI):
            for xi in range(XI):
                value = local[zi, xi] + returned[zi, xi]
                if k < DEGREE - 1:
                    field[k + 1, zi, xi, 8:32, :] = value
                else:
                    for q in range(4):
                        zb, xb = q // 2, q % 2
                        out_ref[zb * ZI + zi, xb * XI + xi] = value[:, 32 * q : 32 * q + 32]
        if k < DEGREE - 1:
            copies = send_halos(k + 1)
            started += copies

    for copy in started:
        copy.wait_send()
    for k in range(DEGREE):
        sent = grouped.at[k, pl.ds(0, BESIDE)]
        pltpu.make_async_copy(sent, sent, sum_send.at[k]).wait()
        pltpu.make_async_copy(sent, sent, spread_send.at[k]).wait()


def shards(sizes, orbitals, potential, projectors, targets, coupling):
    cells = orbitals.transpose(1, 2, 3, 0)
    hbm = pl.BlockSpec(memory_space=pl.ANY)
    vmem = pl.BlockSpec(memory_space=pltpu.VMEM)
    steps = DEGREE
    result = pl.pallas_call(
        functools.partial(kernel, sizes),
        out_shape=jax.ShapeDtypeStruct((CZ, CX, CY, NORB), F32),
        in_specs=[hbm] * 5,
        out_specs=vmem,
        scratch_shapes=[
            pltpu.VMEM((CZ, CX, CY, NORB), F32),
            pltpu.VMEM((PROWS, CZ * CX * CY), F32),
            pltpu.VMEM((CZ * CX, CY), F32),
            pltpu.SMEM((SLOTS,), jnp.int32),
            pltpu.SMEM((ATOM_DEV * NPJ,), F32),
            pltpu.VMEM((steps, ZI, XI, CY + 16, 128), F32),
            pltpu.VMEM((steps, ZI, XI, CY, 128), F32),
            pltpu.VMEM((steps, ZI, XI, CY, 128), F32),
            pltpu.VMEM((steps, ZI, 2, CY, 128), F32),
            pltpu.VMEM((steps, ZI, 2, CY, 128), F32),
            pltpu.VMEM((steps, ZI, CY, 128), F32),
            pltpu.VMEM((steps, ZI, CY, 128), F32),
            pltpu.VMEM((steps, ZI, CY, 128), F32),
            pltpu.VMEM((steps, ZI, CY, 128), F32),
            pltpu.VMEM((steps, BESIDE + 1, 8, 128), F32),
            pltpu.VMEM((steps, BESIDE, 8, 128), F32),
            pltpu.VMEM((steps, 8, 128), F32),
            pltpu.VMEM((steps, 32, 8, 128), F32),
            pltpu.VMEM((4 * PROWS, 384), F32),
            pltpu.VMEM((4 * PROWS, 384), BF16),
            pltpu.VMEM((4 * PROWS, 384), BF16),
            pltpu.VMEM((ROWS, 768), BF16),
            pltpu.VMEM((8 * (BESIDE + 1), 128), F32),
            pltpu.VMEM((PROWS, 256), BF16),
            pltpu.VMEM((2, PROWS, PROWS), BF16),
            pltpu.VMEM((8, 128), F32),
            pltpu.VMEM((ZI, XI, CY, 128), F32),
            pltpu.VMEM((128, 128), F32),
            pltpu.VMEM((ZI, XI, CY, 128), F32),
            pltpu.SemaphoreType.DMA((5,)),
            pltpu.SemaphoreType.DMA((steps, 8)),
            pltpu.SemaphoreType.DMA((steps, 8)),
            pltpu.SemaphoreType.DMA((steps,)),
            pltpu.SemaphoreType.DMA((steps,)),
            pltpu.SemaphoreType.DMA((steps,)),
            pltpu.SemaphoreType.DMA((steps,)),
        ],
        compiler_params=pltpu.CompilerParams(
            collective_id=0, has_side_effects=True, vmem_limit_bytes=60 * 1024 * 1024
        ),
    )(
        cells,
        potential.reshape(CZ * CX, CY),
        projectors.reshape(PROWS, CZ * CX * CY),
        targets.reshape(SLOTS),
        coupling.reshape(ATOM_DEV * NPJ),
    )
    return result.transpose(3, 0, 1, 2)


def solution(mesh):
    sizes = {name: mesh.shape[name] for name in ("gx", "gy", "gz")}
    return jax.shard_map(
        functools.partial(shards, sizes),
        mesh=mesh,
        in_specs=(
            P(None, "gz", "gx", "gy"),
            P("gz", "gx", "gy"),
            P("gz", "gx", "gy", None, None),
            P("gz", "gx", "gy", None),
            P("gz", "gx", "gy", None),
        ),
        out_specs=P(None, "gz", "gx", "gy"),
        check_vma=False,
    )
```

```python
import functools

import jax
import jax.numpy as jnp
from jax import lax
from jax.experimental import pallas as pl
from jax.experimental.pallas import tpu as pltpu
from jax.sharding import PartitionSpec as P

MESH = pl.DeviceIdType.MESH
F32, BF16 = jnp.float32, jnp.bfloat16

DEGREE = 3
NORB, NPJ, SLOTS, ATOM_DEV = 32, 4, 16, 8
CZ, CX, CY = 6, 8, 24
PROWS = SLOTS * NPJ
ZI, XI = CZ // 2, CX // 2
ROWS = ZI * XI * CY
SEG_CELLS = XI * CY

STENCIL = (
    -5369.0 / 1800.0,
    12.0 / 7.0,
    -15.0 / 56.0,
    10.0 / 189.0,
    -1.0 / 112.0,
    2.0 / 1925.0,
    -1.0 / 16632.0,
)
LOWER_EDGE = 2.0
UPPER_EDGE = 16.0
CENTRE = 0.5 * (UPPER_EDGE + LOWER_EDGE)
SPREAD = 0.5 * (UPPER_EDGE - LOWER_EDGE)
WEIGHT = tuple(-0.5 * c / SPREAD for c in STENCIL)

OFFSETS = [
    (a - 1, b - 1, c - 1)
    for a in range(3)
    for b in range(3)
    for c in range(3)
    if (a, b, c) != (1, 1, 1)
]
BESIDE = len(OFFSETS)
RUN = 8


def pick_place(gz, gx, runs, inverse):
    run, y, core = gz // RUN, lax.rem(gz, RUN), lax.rem(gx, 2)
    last = runs - 1
    step = -1 if inverse else 1
    at_end, at_start = y == RUN - 1, y == 0
    upper, lower = core == 1, core == 0
    low, high = run == 0, run == last
    if inverse:
        shift_up, shift_down = at_end & upper & ~low, at_start & lower & ~high
        wrap_up, wrap_down = at_end & lower & low, at_start & upper & high
    else:
        shift_up, shift_down = at_end & upper & ~high, at_start & lower & ~low
        wrap_up, wrap_down = at_end & lower & high, at_start & upper & low
    moved = jnp.where(shift_up | wrap_down, 1, 0) + jnp.where(shift_down | wrap_up, 1, 0)
    runs_on = jnp.where(shift_up, step, jnp.where(shift_down, -step, 0))
    runs_on = jnp.where(wrap_up, -step * last, jnp.where(wrap_down, step * last, runs_on))
    return gz + RUN * runs_on, moved


def split2(value):
    high = value.astype(BF16)
    low = (value - high.astype(F32)).astype(BF16)
    return high, low


def split3(value):
    high = value.astype(BF16)
    rest = value - high.astype(F32)
    mid = rest.astype(BF16)
    low = (rest - mid.astype(F32)).astype(BF16)
    return high, mid, low


def dot(a, b):
    return jnp.dot(a, b, preferred_element_type=F32)


def lanes_of(shape):
    return lax.broadcasted_iota(jnp.int32, shape, len(shape) - 1)


def roll(value, shift):
    return pltpu.roll(value, shift, value.ndim - 1)


def kernel(
    sizes,
    orb_hbm,
    pot_hbm,
    proj_hbm,
    targets_hbm,
    coupling_hbm,
    out_ref,
    orb,
    proj,
    pot_ref,
    targets_ref,
    coupling_ref,
    field,
    z_low,
    z_high,
    x_low,
    x_high,
    x_low_part,
    x_high_part,
    send_low_part,
    send_high_part,
    grouped,
    partials,
    scaled,
    gathered,
    rows_t,
    rows_hi,
    rows_lo,
    columns,
    choose,
    pick,
    overlap,
    factor,
    guest_factor,
    diagonal,
    pot_pad,
    local,
    in_sems,
    halo_send,
    halo_recv,
    sum_send,
    sum_recv,
    spread_send,
    spread_recv,
    factor_sems,
):
    me = {name: lax.axis_index(name) for name in ("gz", "gx", "gy")}

    def beside(offset):
        place = {
            name: lax.rem(me[name] + step + sizes[name], sizes[name])
            for name, step in zip(("gz", "gx", "gy"), offset)
        }
        return (place["gx"], place["gy"], place["gz"])

    runs = sizes["gz"] // RUN

    def host_of(place):
        gz, moved = pick_place(place[2], place[0], runs, False)
        return (place[0], place[1], gz), moved

    targets = [beside(offset) for offset in OFFSETS]
    hosts = [host_of(place) for place in targets]
    my_host, i_moved = host_of((me["gx"], me["gy"], me["gz"]))
    guest_gz, hosting = pick_place(me["gz"], me["gx"], runs, True)
    guest = (me["gx"], me["gy"], guest_gz)
    around_guest = [
        tuple(
            lax.rem(at + step + sizes[name], sizes[name])
            for name, at, step in zip(("gx", "gy", "gz"), guest, (offset[1], offset[2], offset[0]))
        )
        for offset in OFFSETS
    ]

    barrier = pltpu.get_barrier_semaphore()

    def greet(place):
        pl.semaphore_signal(barrier, inc=1, device_id=place, device_id_type=MESH)

    greeted = 27 * hosting + i_moved
    for offset, place, (host, moved) in zip(OFFSETS, targets, hosts):
        direct = 1 if sum(map(abs, offset)) == 1 else 1 - i_moved * moved
        greeted = greeted + moved + direct
        if isinstance(direct, int):
            greet(place)
        else:
            pl.when(direct == 1)(functools.partial(greet, place))
        pl.when(moved == 1)(functools.partial(greet, host))
    pl.when(i_moved == 1)(functools.partial(greet, my_host))

    @pl.when(hosting == 1)
    def _():
        greet(guest)
        for place in around_guest:
            greet(place)

    loads = [
        pltpu.make_async_copy(source, target, in_sems.at[i])
        for i, (source, target) in enumerate(
            (
                (orb_hbm, orb),
                (proj_hbm, proj),
                (targets_hbm, targets_ref),
                (coupling_hbm, coupling_ref),
                (pot_hbm, pot_ref),
            )
        )
    ]
    for load in loads:
        load.start()

    loads[0].wait()
    for zi in range(ZI):
        for xi in range(XI):
            for q in range(4):
                zb, xb = q // 2, q % 2
                field[0, zi, xi, 8:32, 32 * q : 32 * q + 32] = orb[zb * ZI + zi, xb * XI + xi]

    loads[1].wait()
    for q in range(4):
        zb, xb = q // 2, q % 2
        for zi in range(ZI):
            start = (zb * ZI + zi) * CX * CY + xb * SEG_CELLS
            rows_t[PROWS * q : PROWS * (q + 1), SEG_CELLS * zi : SEG_CELLS * (zi + 1)] = proj[
                :, start : start + SEG_CELLS
            ]
    rows_t[:, ROWS:384] = jnp.zeros((4 * PROWS, 384 - ROWS), F32)
    high, low = split2(rows_t[...])
    rows_hi[...] = high
    rows_lo[...] = low

    loads[2].wait()
    loads[3].wait()
    lane_slot = lanes_of((8, 128)) % PROWS // NPJ
    row_slot = lax.broadcasted_iota(jnp.int32, (PROWS, 256), 0) // NPJ
    named_lane = jnp.zeros((8, 128), jnp.int32)
    named_row = jnp.zeros((PROWS, 256), jnp.int32)
    own_first = ATOM_DEV * (BESIDE // 2)
    for s in range(SLOTS):
        atom = targets_ref[s]
        atom = jnp.where(
            atom < own_first,
            atom,
            jnp.where(atom < own_first + ATOM_DEV, atom + own_first, atom - ATOM_DEV),
        )
        named_lane = jnp.where(lane_slot == s, atom, named_lane)
        named_row = jnp.where(row_slot == s, atom, named_row)
    atom_row = lax.broadcasted_iota(jnp.int32, (8, 128), 0)
    for j in range(BESIDE + 1):
        choose[8 * j : 8 * j + 8, :] = jnp.where(named_lane == atom_row + 8 * j, 1.0, 0.0)
    pick[...] = jnp.where(named_row == lanes_of((PROWS, 256)), 1.0, 0.0).astype(BF16)
    for k in range(DEGREE):
        for j in range(BESIDE + 1, 32):
            gathered[k, j] = jnp.zeros((8, 128), F32)
    pair = NPJ * lax.broadcasted_iota(jnp.int32, (8, 128), 0) + lanes_of((8, 128)) // NORB
    weights = jnp.zeros((8, 128), F32)
    for j in range(ATOM_DEV * NPJ):
        weights = jnp.where(pair == j, coupling_ref[j], weights)
    factor[...] = weights * (1.0 / SPREAD)

    group = lanes_of((PROWS, 128)) // NORB
    own_group = group == lax.broadcasted_iota(jnp.int32, (PROWS, 128), 0) % NPJ
    is_x1 = lanes_of((CY, 128)) % 64 >= 32
    is_z1 = lanes_of((CY, 128)) >= 64

    def everywhere(masked):
        paired = masked + roll(masked, 64)
        return paired + roll(paired, 32)

    def products(cells):
        f_hi, f_lo = split2(cells.reshape(ROWS, 128))
        p_hi, p_lo = rows_hi[:, :ROWS], rows_lo[:, :ROWS]
        crossed = dot(p_hi, f_hi) + (dot(p_lo, f_hi) + dot(p_hi, f_lo))
        kept = crossed[3 * PROWS :]
        for q in range(3):
            kept = jnp.where(group == q, crossed[PROWS * q : PROWS * (q + 1)], kept)
        return everywhere(kept)

    def group_sums(k, by_row):
        stacked = jnp.concatenate(split2(jnp.where(own_group, by_row, 0.0)), axis=0)
        grouped[k] = dot(choose[...].astype(BF16), stacked).reshape(BESIDE + 1, 8, 128)

    def send_sums(k):
        for j, (place, moved) in enumerate(hosts):
            pltpu.make_async_remote_copy(
                src_ref=grouped.at[k, j],
                dst_ref=partials.at[k, j + BESIDE * moved],
                send_sem=sum_send.at[k, 0],
                recv_sem=sum_recv.at[k, moved],
                device_id=place,
                device_id_type=MESH,
            ).start()

        @pl.when(i_moved == 1)
        def _():
            own_sums(k).start()

    def own_sums(k):
        return pltpu.make_async_remote_copy(
            src_ref=grouped.at[k, BESIDE],
            dst_ref=partials.at[k, 2 * BESIDE],
            send_sem=sum_send.at[k, 1],
            recv_sem=sum_recv.at[k, 1],
            device_id=my_host,
            device_id_type=MESH,
        )

    def send_factor():
        return pltpu.make_async_remote_copy(
            src_ref=factor,
            dst_ref=guest_factor,
            send_sem=factor_sems.at[0],
            recv_sem=factor_sems.at[1],
            device_id=my_host,
            device_id_type=MESH,
        )

    def halo_copies(k):
        own = field.at[k, :, :, pl.ds(8, CY), :]
        moves = (
            (own, z_low.at[k], (1, 0, 0)),
            (own, z_high.at[k], (-1, 0, 0)),
            (field.at[k, :, :, pl.ds(24, 8), :], field.at[k, :, :, pl.ds(0, 8), :], (0, 0, 1)),
            (field.at[k, :, :, pl.ds(8, 8), :], field.at[k, :, :, pl.ds(32, 8), :], (0, 0, -1)),
            (field.at[k, :, pl.ds(2, 2), pl.ds(8, CY), :], x_low.at[k], (0, 1, 0)),
            (field.at[k, :, pl.ds(0, 2), pl.ds(8, CY), :], x_high.at[k], (0, -1, 0)),
            (send_low_part.at[k], x_low_part.at[k], (0, 1, 0)),
            (send_high_part.at[k], x_high_part.at[k], (0, -1, 0)),
        )
        return [
            pltpu.make_async_remote_copy(
                src_ref=source,
                dst_ref=target,
                send_sem=halo_send.at[k, i],
                recv_sem=halo_recv.at[k, i],
                device_id=beside(offset),
                device_id_type=MESH,
            )
            for i, (source, target, offset) in enumerate(moves)
        ]

    def send_halos(k):
        for zi in range(ZI):
            cell = [field[k, zi, xi, 8:32, :] for xi in range(XI)]
            send_low_part[k, zi] = jnp.where(is_x1, cell[1], roll(cell[0], 96))
            send_high_part[k, zi] = jnp.where(is_x1, roll(cell[2], 32), cell[3])
        copies = halo_copies(k)
        for copy in copies:
            copy.start()
        return copies

    def fill_overlap():
        o_hi, o_lo = split2(proj[...])

        def rows_by_rows(a, b):
            return lax.dot_general(a, b, (((1,), (1,)), ((), ())), preferred_element_type=F32)

        gram = rows_by_rows(o_hi, o_hi) + (rows_by_rows(o_hi, o_lo) + rows_by_rows(o_lo, o_hi))
        g_hi, g_lo = split2(gram)
        overlap[0] = g_hi
        overlap[1] = g_lo

    loads[4].wait()
    pot_pad[...] = jnp.zeros((128, 128), F32)
    pot_pad[: CZ * CX, :CY] = pot_ref[...]
    pot_t = pot_pad[...].T[:CY]
    pieces = split3(pot_t)
    stacked_pot = jnp.concatenate([p.astype(F32) for p in pieces], axis=0).astype(BF16)
    plane = lax.broadcasted_iota(jnp.int32, (128, 128), 0)
    lane = lanes_of((128, 128))
    wanted = (lane // 64 * ZI) * CX + lane // 32 % 2 * XI

    def fill_diagonal():
        for zi in range(ZI):
            for xi in range(XI):
                hot = jnp.where(plane == wanted + (zi * CX + xi), 1.0, 0.0).astype(BF16)
                got = dot(stacked_pot, hot)
                value = got[:CY] + (got[CY : 2 * CY] + got[2 * CY :])
                diagonal[zi, xi] = (value - (CENTRE + 1.5 * STENCIL[0])) * (1.0 / SPREAD)

    def fill_columns():
        transposed = rows_t[...].T[:ROWS]
        t_hi, t_lo = split2(transposed)
        columns[:, 0:256] = t_hi
        columns[:, 256:512] = t_lo
        columns[:, 512:768] = t_hi

    def spread(k, which, place, slot):
        return pltpu.make_async_remote_copy(
            src_ref=scaled.at[k, which],
            dst_ref=gathered.at[k, slot],
            send_sem=spread_send.at[k, which],
            recv_sem=spread_recv.at[k, 0 if slot < BESIDE else 1],
            device_id=place,
            device_id_type=MESH,
        )

    def send_atoms(k):
        @pl.when(i_moved == 0)
        def _():
            landed = partials.at[k, pl.ds(0, BESIDE)]
            pltpu.make_async_copy(landed, landed, sum_recv.at[k, 0]).wait()
            total = grouped[k, BESIDE]
            for j in range(BESIDE):
                total = total + partials[k, j]
            total = total * factor[...]
            scaled[k, 0] = total
            for j, place in enumerate(targets):
                spread(k, 0, place, BESIDE - 1 - j).start()
            gathered[k, BESIDE] = total

        @pl.when(hosting == 1)
        def _():
            landed = partials.at[k, pl.ds(BESIDE, BESIDE + 1)]
            pltpu.make_async_copy(landed, landed, sum_recv.at[k, 1]).wait()
            if k == 0:
                send_factor().wait_recv()
            total = partials[k, 2 * BESIDE]
            for j in range(BESIDE, 2 * BESIDE):
                total = total + partials[k, j]
            scaled[k, 1] = total * guest_factor[...]
            for j, place in enumerate(around_guest):
                spread(k, 1, place, BESIDE - 1 - j).start()
            spread(k, 1, guest, BESIDE).start()

    def stencil(k, copies):
        for copy in copies:
            copy.wait_recv()
        for xi in range(XI):
            own = [field[k, zi, xi, 8:32, :] for zi in range(ZI)]
            low = [z_low[k, zi, xi] for zi in range(ZI)]
            high = [z_high[k, zi, xi] for zi in range(ZI)]
            before = [roll(jnp.where(is_z1, l, o), 64) for o, l in zip(own, low)]
            after = [roll(jnp.where(is_z1, o, h), 64) for o, h in zip(own, high)]
            line = low + before + own + after + high
            for zi in range(ZI):
                at = zi + 2 * ZI
                total = diagonal[zi, xi] * own[zi]
                for d in range(1, 7):
                    total = total + WEIGHT[d] * (line[at - d] + line[at + d])
                for d in range(1, 7):
                    total = total + WEIGHT[d] * (
                        field[k, zi, xi, 8 - d : 32 - d, :] + field[k, zi, xi, 8 + d : 32 + d, :]
                    )
                local[zi, xi] = total
        for zi in range(ZI):
            own = [field[k, zi, xi, 8:32, :] for xi in range(XI)]
            up = [roll(o, 32) for o in own]
            down = [roll(o, 96) for o in own]
            low = [x_low[k, zi, i] for i in range(2)]
            high = [x_high[k, zi, i] for i in range(2)]
            low_part, high_part = x_low_part[k, zi], x_high_part[k, zi]
            before = [
                jnp.where(is_x1, up[0], low_part),
                jnp.where(is_x1, up[1], roll(low_part, 96)),
                jnp.where(is_x1, up[2], roll(low[0], 96)),
                jnp.where(is_x1, up[3], roll(low[1], 96)),
            ]
            after = [
                jnp.where(is_x1, roll(high[0], 32), down[0]),
                jnp.where(is_x1, roll(high[1], 32), down[1]),
                jnp.where(is_x1, high_part, down[2]),
                jnp.where(is_x1, roll(high_part, 32), down[3]),
            ]
            line = low + before + own + after + high
            for xi in range(XI):
                at = xi + 6
                total = local[zi, xi]
                for d in range(1, 7):
                    total = total + WEIGHT[d] * (line[at - d] + line[at + d])
                local[zi, xi] = total

    def scale_local(k):
        if k > 0:
            for zi in range(ZI):
                for xi in range(XI):
                    local[zi, xi] = 2.0 * local[zi, xi] - field[k - 1, zi, xi, 8:32, :]

    def picked_rows(k):
        landed = gathered.at[k, pl.ds(0, BESIDE)]
        pltpu.make_async_copy(landed, landed, spread_recv.at[k, 0]).wait()

        @pl.when(i_moved == 1)
        def _():
            own = gathered.at[k, BESIDE]
            pltpu.make_async_copy(own, own, spread_recv.at[k, 1]).wait()

        a, b = split2(gathered[k].reshape(256, 128))
        hot = pick[...]
        picked = dot(hot, a) + dot(hot, b)
        rep = everywhere(jnp.where(own_group, picked, 0.0))
        return rep if k == 0 else 2.0 * rep

    def projected(rep):
        r_hi, r_lo = split2(rep)
        return dot(overlap[0], r_hi) + (dot(overlap[1], r_hi) + dot(overlap[0], r_lo))

    def nonlocal_part(rep):
        blocks = jnp.concatenate([jnp.where(group == q, rep, 0.0) for q in range(4)], axis=0)
        b_hi, b_lo = split2(blocks)
        return dot(columns[...], jnp.concatenate([b_hi, b_hi, b_lo], axis=0))

    group_sums(0, products(field[0, :, :, 8:32, :]))
    pl.semaphore_wait(barrier, greeted)
    send_sums(0)

    @pl.when(i_moved == 1)
    def _():
        send_factor().start()

    copies = send_halos(0)
    started = list(copies)
    fill_diagonal()
    fill_columns()
    fill_overlap()
    for k in range(DEGREE):
        send_atoms(k)
        stencil(k, copies)
        scale_local(k)
        if k < DEGREE - 1:
            ready = products(local[...])
        rep = picked_rows(k)
        if k < DEGREE - 1:
            group_sums(k + 1, ready + projected(rep))
            send_sums(k + 1)
        returned = nonlocal_part(rep).reshape(ZI, XI, CY, 128)
        for zi in range(ZI):
            for xi in range(XI):
                value = local[zi, xi] + returned[zi, xi]
                if k < DEGREE - 1:
                    field[k + 1, zi, xi, 8:32, :] = value
                else:
                    for q in range(4):
                        zb, xb = q // 2, q % 2
                        out_ref[zb * ZI + zi, xb * XI + xi] = value[:, 32 * q : 32 * q + 32]
        if k < DEGREE - 1:
            copies = send_halos(k + 1)
            started += copies

    for copy in started:
        copy.wait_send()
    for k in range(DEGREE):
        sent = grouped.at[k, pl.ds(0, BESIDE)]
        pltpu.make_async_copy(sent, sent, sum_send.at[k, 0]).wait()

        @pl.when(i_moved == 0)
        def _():
            pltpu.make_async_copy(sent, sent, spread_send.at[k, 0]).wait()

        @pl.when(i_moved == 1)
        def _():
            own_sums(k).wait_send()

        @pl.when(hosting == 1)
        def _():
            whole = grouped.at[k]
            pltpu.make_async_copy(whole, whole, spread_send.at[k, 1]).wait()

    @pl.when(i_moved == 1)
    def _():
        send_factor().wait_send()


def shards(sizes, orbitals, potential, projectors, targets, coupling):
    cells = orbitals.transpose(1, 2, 3, 0)
    hbm = pl.BlockSpec(memory_space=pl.ANY)
    vmem = pl.BlockSpec(memory_space=pltpu.VMEM)
    steps = DEGREE
    result = pl.pallas_call(
        functools.partial(kernel, sizes),
        out_shape=jax.ShapeDtypeStruct((CZ, CX, CY, NORB), F32),
        in_specs=[hbm] * 5,
        out_specs=vmem,
        scratch_shapes=[
            pltpu.VMEM((CZ, CX, CY, NORB), F32),
            pltpu.VMEM((PROWS, CZ * CX * CY), F32),
            pltpu.VMEM((CZ * CX, CY), F32),
            pltpu.SMEM((SLOTS,), jnp.int32),
            pltpu.SMEM((ATOM_DEV * NPJ,), F32),
            pltpu.VMEM((steps, ZI, XI, CY + 16, 128), F32),
            pltpu.VMEM((steps, ZI, XI, CY, 128), F32),
            pltpu.VMEM((steps, ZI, XI, CY, 128), F32),
            pltpu.VMEM((steps, ZI, 2, CY, 128), F32),
            pltpu.VMEM((steps, ZI, 2, CY, 128), F32),
            pltpu.VMEM((steps, ZI, CY, 128), F32),
            pltpu.VMEM((steps, ZI, CY, 128), F32),
            pltpu.VMEM((steps, ZI, CY, 128), F32),
            pltpu.VMEM((steps, ZI, CY, 128), F32),
            pltpu.VMEM((steps, BESIDE + 1, 8, 128), F32),
            pltpu.VMEM((steps, 2 * BESIDE + 1, 8, 128), F32),
            pltpu.VMEM((steps, 2, 8, 128), F32),
            pltpu.VMEM((steps, 32, 8, 128), F32),
            pltpu.VMEM((4 * PROWS, 384), F32),
            pltpu.VMEM((4 * PROWS, 384), BF16),
            pltpu.VMEM((4 * PROWS, 384), BF16),
            pltpu.VMEM((ROWS, 768), BF16),
            pltpu.VMEM((8 * (BESIDE + 1), 128), F32),
            pltpu.VMEM((PROWS, 256), BF16),
            pltpu.VMEM((2, PROWS, PROWS), BF16),
            pltpu.VMEM((8, 128), F32),
            pltpu.VMEM((8, 128), F32),
            pltpu.VMEM((ZI, XI, CY, 128), F32),
            pltpu.VMEM((128, 128), F32),
            pltpu.VMEM((ZI, XI, CY, 128), F32),
            pltpu.SemaphoreType.DMA((5,)),
            pltpu.SemaphoreType.DMA((steps, 8)),
            pltpu.SemaphoreType.DMA((steps, 8)),
            pltpu.SemaphoreType.DMA((steps, 2)),
            pltpu.SemaphoreType.DMA((steps, 2)),
            pltpu.SemaphoreType.DMA((steps, 2)),
            pltpu.SemaphoreType.DMA((steps, 2)),
            pltpu.SemaphoreType.DMA((2,)),
        ],
        compiler_params=pltpu.CompilerParams(
            collective_id=0, has_side_effects=True, vmem_limit_bytes=60 * 1024 * 1024
        ),
    )(
        cells,
        potential.reshape(CZ * CX, CY),
        projectors.reshape(PROWS, CZ * CX * CY),
        targets.reshape(SLOTS),
        coupling.reshape(ATOM_DEV * NPJ),
    )
    return result.transpose(3, 0, 1, 2)


def solution(mesh):
    sizes = {name: mesh.shape[name] for name in ("gx", "gy", "gz")}
    return jax.shard_map(
        functools.partial(shards, sizes),
        mesh=mesh,
        in_specs=(
            P(None, "gz", "gx", "gy"),
            P("gz", "gx", "gy"),
            P("gz", "gx", "gy", None, None),
            P("gz", "gx", "gy", None),
            P("gz", "gx", "gy", None),
        ),
        out_specs=P(None, "gz", "gx", "gy"),
        check_vma=False,
    )
```

```python
import functools

import jax
import jax.numpy as jnp
from jax import lax
from jax.experimental import pallas as pl
from jax.experimental.pallas import tpu as pltpu
from jax.sharding import PartitionSpec as P

MESH = pl.DeviceIdType.MESH
F32, BF16 = jnp.float32, jnp.bfloat16

DEGREE = 3
NORB, NPJ, SLOTS, ATOM_DEV = 32, 4, 16, 8
CZ, CX, CY = 6, 8, 24
PROWS = SLOTS * NPJ
ZI, XI = CZ // 2, CX // 2
ROWS = ZI * XI * CY
SEG_CELLS = XI * CY

STENCIL = (
    -5369.0 / 1800.0,
    12.0 / 7.0,
    -15.0 / 56.0,
    10.0 / 189.0,
    -1.0 / 112.0,
    2.0 / 1925.0,
    -1.0 / 16632.0,
)
LOWER_EDGE = 2.0
UPPER_EDGE = 16.0
CENTRE = 0.5 * (UPPER_EDGE + LOWER_EDGE)
SPREAD = 0.5 * (UPPER_EDGE - LOWER_EDGE)
WEIGHT = tuple(-0.5 * c / SPREAD for c in STENCIL)

OFFSETS = [
    (a - 1, b - 1, c - 1)
    for a in range(3)
    for b in range(3)
    for c in range(3)
    if (a, b, c) != (1, 1, 1)
]
BESIDE = len(OFFSETS)
RUN = 8


def pick_place(gz, gx, runs, inverse):
    run, y, core = gz // RUN, lax.rem(gz, RUN), lax.rem(gx, 2)
    last = runs - 1
    step = -1 if inverse else 1
    at_end, at_start = y == RUN - 1, y == 0
    upper, lower = core == 1, core == 0
    low, high = run == 0, run == last
    if inverse:
        shift_up, shift_down = at_end & upper & ~low, at_start & lower & ~high
        wrap_up, wrap_down = at_end & lower & low, at_start & upper & high
    else:
        shift_up, shift_down = at_end & upper & ~high, at_start & lower & ~low
        wrap_up, wrap_down = at_end & lower & high, at_start & upper & low
    moved = jnp.where(shift_up | wrap_down, 1, 0) + jnp.where(shift_down | wrap_up, 1, 0)
    runs_on = jnp.where(shift_up, step, jnp.where(shift_down, -step, 0))
    runs_on = jnp.where(wrap_up, -step * last, jnp.where(wrap_down, step * last, runs_on))
    return gz + RUN * runs_on, moved


def split2(value):
    high = value.astype(BF16)
    low = (value - high.astype(F32)).astype(BF16)
    return high, low


def split3(value):
    high = value.astype(BF16)
    rest = value - high.astype(F32)
    mid = rest.astype(BF16)
    low = (rest - mid.astype(F32)).astype(BF16)
    return high, mid, low


def dot(a, b):
    return jnp.dot(a, b, preferred_element_type=F32)


def lanes_of(shape):
    return lax.broadcasted_iota(jnp.int32, shape, len(shape) - 1)


def roll(value, shift):
    return pltpu.roll(value, shift, value.ndim - 1)


def kernel(
    sizes,
    orb_hbm,
    pot_hbm,
    proj_hbm,
    targets_hbm,
    coupling_hbm,
    out_ref,
    orb,
    proj,
    pot_ref,
    targets_ref,
    coupling_ref,
    field,
    z_low,
    z_high,
    x_low,
    x_high,
    x_low_part,
    x_high_part,
    send_low_part,
    send_high_part,
    grouped,
    partials,
    scaled,
    gathered,
    rows_t,
    rows_hi,
    rows_lo,
    columns,
    choose,
    pick,
    overlap,
    factor,
    guest_factor,
    diagonal,
    pot_pad,
    local,
    in_sems,
    halo_send,
    halo_recv,
    sum_send,
    sum_recv,
    spread_send,
    spread_recv,
    factor_sems,
):
    me = {name: lax.axis_index(name) for name in ("gz", "gx", "gy")}

    def beside(offset):
        place = {
            name: lax.rem(me[name] + step + sizes[name], sizes[name])
            for name, step in zip(("gz", "gx", "gy"), offset)
        }
        return (place["gx"], place["gy"], place["gz"])

    runs = sizes["gz"] // RUN

    def host_of(place):
        gz, moved = pick_place(place[2], place[0], runs, False)
        return (place[0], place[1], gz), moved

    targets = [beside(offset) for offset in OFFSETS]
    hosts = [host_of(place) for place in targets]
    my_host, i_moved = host_of((me["gx"], me["gy"], me["gz"]))
    guest_gz, hosting = pick_place(me["gz"], me["gx"], runs, True)
    guest = (me["gx"], me["gy"], guest_gz)
    around_guest = [
        tuple(
            lax.rem(at + step + sizes[name], sizes[name])
            for name, at, step in zip(("gx", "gy", "gz"), guest, (offset[1], offset[2], offset[0]))
        )
        for offset in OFFSETS
    ]

    barrier = pltpu.get_barrier_semaphore()

    def greet(place):
        pl.semaphore_signal(barrier, inc=1, device_id=place, device_id_type=MESH)

    greeted = 27 * hosting + i_moved
    for offset, place, (host, moved) in zip(OFFSETS, targets, hosts):
        direct = 1 if sum(map(abs, offset)) == 1 else 1 - i_moved * moved
        greeted = greeted + moved + direct
        if isinstance(direct, int):
            greet(place)
        else:
            pl.when(direct == 1)(functools.partial(greet, place))
        pl.when(moved == 1)(functools.partial(greet, host))
    pl.when(i_moved == 1)(functools.partial(greet, my_host))

    @pl.when(hosting == 1)
    def _():
        greet(guest)
        for place in around_guest:
            greet(place)

    loads = [
        pltpu.make_async_copy(source, target, in_sems.at[i])
        for i, (source, target) in enumerate(
            (
                (orb_hbm, orb),
                (proj_hbm, proj),
                (targets_hbm, targets_ref),
                (coupling_hbm, coupling_ref),
                (pot_hbm, pot_ref),
            )
        )
    ]
    for load in loads:
        load.start()

    loads[0].wait()
    for zi in range(ZI):
        for xi in range(XI):
            for q in range(4):
                zb, xb = q // 2, q % 2
                field[0, zi, xi, 8:32, 32 * q : 32 * q + 32] = orb[zb * ZI + zi, xb * XI + xi]

    loads[1].wait()
    for q in range(4):
        zb, xb = q // 2, q % 2
        for zi in range(ZI):
            start = (zb * ZI + zi) * CX * CY + xb * SEG_CELLS
            rows_t[PROWS * q : PROWS * (q + 1), SEG_CELLS * zi : SEG_CELLS * (zi + 1)] = proj[
                :, start : start + SEG_CELLS
            ]
    rows_t[:, ROWS:384] = jnp.zeros((4 * PROWS, 384 - ROWS), F32)
    high, low = split2(rows_t[...])
    rows_hi[...] = high
    rows_lo[...] = low

    loads[2].wait()
    loads[3].wait()
    lane_slot = lanes_of((8, 128)) % PROWS // NPJ
    row_slot = lax.broadcasted_iota(jnp.int32, (PROWS, 256), 0) // NPJ
    named_lane = jnp.zeros((8, 128), jnp.int32)
    named_row = jnp.zeros((PROWS, 256), jnp.int32)
    own_first = ATOM_DEV * (BESIDE // 2)
    for s in range(SLOTS):
        atom = targets_ref[s]
        atom = jnp.where(
            atom < own_first,
            atom,
            jnp.where(atom < own_first + ATOM_DEV, atom + own_first, atom - ATOM_DEV),
        )
        named_lane = jnp.where(lane_slot == s, atom, named_lane)
        named_row = jnp.where(row_slot == s, atom, named_row)
    atom_row = lax.broadcasted_iota(jnp.int32, (8, 128), 0)
    for j in range(BESIDE + 1):
        choose[8 * j : 8 * j + 8, :] = jnp.where(named_lane == atom_row + 8 * j, 1.0, 0.0)
    pick[...] = jnp.where(named_row == lanes_of((PROWS, 256)), 1.0, 0.0).astype(BF16)
    for k in range(DEGREE):
        for j in range(BESIDE + 1, 32):
            gathered[k, j] = jnp.zeros((8, 128), F32)
    pair = NPJ * lax.broadcasted_iota(jnp.int32, (8, 128), 0) + lanes_of((8, 128)) // NORB
    weights = jnp.zeros((8, 128), F32)
    for j in range(ATOM_DEV * NPJ):
        weights = jnp.where(pair == j, coupling_ref[j], weights)
    factor[...] = weights * (1.0 / SPREAD)

    group = lanes_of((PROWS, 128)) // NORB
    own_group = group == lax.broadcasted_iota(jnp.int32, (PROWS, 128), 0) % NPJ
    is_x1 = lanes_of((CY, 128)) % 64 >= 32
    is_z1 = lanes_of((CY, 128)) >= 64

    def everywhere(masked):
        paired = masked + roll(masked, 64)
        return paired + roll(paired, 32)

    def products(cells):
        f_hi, f_lo = split2(cells.reshape(ROWS, 128))
        p_hi, p_lo = rows_hi[:, :ROWS], rows_lo[:, :ROWS]
        crossed = dot(p_hi, f_hi) + (dot(p_lo, f_hi) + dot(p_hi, f_lo))
        kept = crossed[3 * PROWS :]
        for q in range(3):
            kept = jnp.where(group == q, crossed[PROWS * q : PROWS * (q + 1)], kept)
        return everywhere(kept)

    def group_sums(k, by_row):
        stacked = jnp.concatenate(split2(jnp.where(own_group, by_row, 0.0)), axis=0)
        grouped[k] = dot(choose[...].astype(BF16), stacked).reshape(BESIDE + 1, 8, 128)

    def send_sums(k):
        for j, (place, moved) in enumerate(hosts):
            pltpu.make_async_remote_copy(
                src_ref=grouped.at[k, j],
                dst_ref=partials.at[k, j + BESIDE * moved],
                send_sem=sum_send.at[k, 0],
                recv_sem=sum_recv.at[k, moved],
                device_id=place,
                device_id_type=MESH,
            ).start()

        @pl.when(i_moved == 1)
        def _():
            own_sums(k).start()

    def own_sums(k):
        return pltpu.make_async_remote_copy(
            src_ref=grouped.at[k, BESIDE],
            dst_ref=partials.at[k, 2 * BESIDE],
            send_sem=sum_send.at[k, 1],
            recv_sem=sum_recv.at[k, 1],
            device_id=my_host,
            device_id_type=MESH,
        )

    def send_factor():
        return pltpu.make_async_remote_copy(
            src_ref=factor,
            dst_ref=guest_factor,
            send_sem=factor_sems.at[0],
            recv_sem=factor_sems.at[1],
            device_id=my_host,
            device_id_type=MESH,
        )

    def halo_copies(k):
        own = field.at[k, :, :, pl.ds(8, CY), :]
        moves = (
            (own, z_low.at[k], (1, 0, 0)),
            (own, z_high.at[k], (-1, 0, 0)),
            (field.at[k, :, :, pl.ds(24, 8), :], field.at[k, :, :, pl.ds(0, 8), :], (0, 0, 1)),
            (field.at[k, :, :, pl.ds(8, 8), :], field.at[k, :, :, pl.ds(32, 8), :], (0, 0, -1)),
            (field.at[k, :, pl.ds(2, 2), pl.ds(8, CY), :], x_low.at[k], (0, 1, 0)),
            (field.at[k, :, pl.ds(0, 2), pl.ds(8, CY), :], x_high.at[k], (0, -1, 0)),
            (send_low_part.at[k], x_low_part.at[k], (0, 1, 0)),
            (send_high_part.at[k], x_high_part.at[k], (0, -1, 0)),
        )
        return [
            pltpu.make_async_remote_copy(
                src_ref=source,
                dst_ref=target,
                send_sem=halo_send.at[k, i],
                recv_sem=halo_recv.at[k, i],
                device_id=beside(offset),
                device_id_type=MESH,
            )
            for i, (source, target, offset) in enumerate(moves)
        ]

    def send_halos(k):
        for zi in range(ZI):
            cell = [field[k, zi, xi, 8:32, :] for xi in range(XI)]
            send_low_part[k, zi] = jnp.where(is_x1, cell[1], roll(cell[0], 96))
            send_high_part[k, zi] = jnp.where(is_x1, roll(cell[2], 32), cell[3])
        copies = halo_copies(k)
        for copy in copies[2:]:
            copy.start()
        return copies

    def fill_overlap():
        o_hi, o_lo = split2(proj[...])

        def rows_by_rows(a, b):
            return lax.dot_general(a, b, (((1,), (1,)), ((), ())), preferred_element_type=F32)

        gram = rows_by_rows(o_hi, o_hi) + (rows_by_rows(o_hi, o_lo) + rows_by_rows(o_lo, o_hi))
        g_hi, g_lo = split2(gram)
        overlap[0] = g_hi
        overlap[1] = g_lo

    loads[4].wait()
    pot_pad[...] = jnp.zeros((128, 128), F32)
    pot_pad[: CZ * CX, :CY] = pot_ref[...]
    pot_t = pot_pad[...].T[:CY]
    pieces = split3(pot_t)
    stacked_pot = jnp.concatenate([p.astype(F32) for p in pieces], axis=0).astype(BF16)
    plane = lax.broadcasted_iota(jnp.int32, (128, 128), 0)
    lane = lanes_of((128, 128))
    wanted = (lane // 64 * ZI) * CX + lane // 32 % 2 * XI

    def fill_diagonal():
        for zi in range(ZI):
            for xi in range(XI):
                hot = jnp.where(plane == wanted + (zi * CX + xi), 1.0, 0.0).astype(BF16)
                got = dot(stacked_pot, hot)
                value = got[:CY] + (got[CY : 2 * CY] + got[2 * CY :])
                diagonal[zi, xi] = (value - (CENTRE + 1.5 * STENCIL[0])) * (1.0 / SPREAD)

    def fill_columns():
        transposed = rows_t[...].T[:ROWS]
        t_hi, t_lo = split2(transposed)
        columns[:, 0:256] = t_hi
        columns[:, 256:512] = t_lo
        columns[:, 512:768] = t_hi

    def spread(k, which, place, slot):
        return pltpu.make_async_remote_copy(
            src_ref=scaled.at[k, which],
            dst_ref=gathered.at[k, slot],
            send_sem=spread_send.at[k, which],
            recv_sem=spread_recv.at[k, 0 if slot < BESIDE else 1],
            device_id=place,
            device_id_type=MESH,
        )

    def send_atoms(k, copies):
        for copy in copies[2:4]:
            copy.wait_recv()
        for copy in copies[:2]:
            copy.start()
        @pl.when(i_moved == 0)
        def _():
            landed = partials.at[k, pl.ds(0, BESIDE)]
            pltpu.make_async_copy(landed, landed, sum_recv.at[k, 0]).wait()
            total = grouped[k, BESIDE]
            for j in range(BESIDE):
                total = total + partials[k, j]
            total = total * factor[...]
            scaled[k, 0] = total
            for j, place in enumerate(targets):
                spread(k, 0, place, BESIDE - 1 - j).start()
            gathered[k, BESIDE] = total

        @pl.when(hosting == 1)
        def _():
            landed = partials.at[k, pl.ds(BESIDE, BESIDE + 1)]
            pltpu.make_async_copy(landed, landed, sum_recv.at[k, 1]).wait()
            if k == 0:
                send_factor().wait_recv()
            total = partials[k, 2 * BESIDE]
            for j in range(BESIDE, 2 * BESIDE):
                total = total + partials[k, j]
            scaled[k, 1] = total * guest_factor[...]
            for j, place in enumerate(around_guest):
                spread(k, 1, place, BESIDE - 1 - j).start()
            spread(k, 1, guest, BESIDE).start()

    def stencil(k, copies):
        for copy in copies[:2] + copies[4:]:
            copy.wait_recv()
        for xi in range(XI):
            own = [field[k, zi, xi, 8:32, :] for zi in range(ZI)]
            low = [z_low[k, zi, xi] for zi in range(ZI)]
            high = [z_high[k, zi, xi] for zi in range(ZI)]
            before = [roll(jnp.where(is_z1, l, o), 64) for o, l in zip(own, low)]
            after = [roll(jnp.where(is_z1, o, h), 64) for o, h in zip(own, high)]
            line = low + before + own + after + high
            for zi in range(ZI):
                at = zi + 2 * ZI
                total = diagonal[zi, xi] * own[zi]
                for d in range(1, 7):
                    total = total + WEIGHT[d] * (line[at - d] + line[at + d])
                for d in range(1, 7):
                    total = total + WEIGHT[d] * (
                        field[k, zi, xi, 8 - d : 32 - d, :] + field[k, zi, xi, 8 + d : 32 + d, :]
                    )
                local[zi, xi] = total
        for zi in range(ZI):
            own = [field[k, zi, xi, 8:32, :] for xi in range(XI)]
            up = [roll(o, 32) for o in own]
            down = [roll(o, 96) for o in own]
            low = [x_low[k, zi, i] for i in range(2)]
            high = [x_high[k, zi, i] for i in range(2)]
            low_part, high_part = x_low_part[k, zi], x_high_part[k, zi]
            before = [
                jnp.where(is_x1, up[0], low_part),
                jnp.where(is_x1, up[1], roll(low_part, 96)),
                jnp.where(is_x1, up[2], roll(low[0], 96)),
                jnp.where(is_x1, up[3], roll(low[1], 96)),
            ]
            after = [
                jnp.where(is_x1, roll(high[0], 32), down[0]),
                jnp.where(is_x1, roll(high[1], 32), down[1]),
                jnp.where(is_x1, high_part, down[2]),
                jnp.where(is_x1, roll(high_part, 32), down[3]),
            ]
            line = low + before + own + after + high
            for xi in range(XI):
                at = xi + 6
                total = local[zi, xi]
                for d in range(1, 7):
                    total = total + WEIGHT[d] * (line[at - d] + line[at + d])
                local[zi, xi] = total

    def scale_local(k):
        if k > 0:
            for zi in range(ZI):
                for xi in range(XI):
                    local[zi, xi] = 2.0 * local[zi, xi] - field[k - 1, zi, xi, 8:32, :]

    def picked_rows(k):
        landed = gathered.at[k, pl.ds(0, BESIDE)]
        pltpu.make_async_copy(landed, landed, spread_recv.at[k, 0]).wait()

        @pl.when(i_moved == 1)
        def _():
            own = gathered.at[k, BESIDE]
            pltpu.make_async_copy(own, own, spread_recv.at[k, 1]).wait()

        a, b = split2(gathered[k].reshape(256, 128))
        hot = pick[...]
        picked = dot(hot, a) + dot(hot, b)
        rep = everywhere(jnp.where(own_group, picked, 0.0))
        return rep if k == 0 else 2.0 * rep

    def projected(rep):
        r_hi, r_lo = split2(rep)
        return dot(overlap[0], r_hi) + (dot(overlap[1], r_hi) + dot(overlap[0], r_lo))

    def nonlocal_part(rep):
        blocks = jnp.concatenate([jnp.where(group == q, rep, 0.0) for q in range(4)], axis=0)
        b_hi, b_lo = split2(blocks)
        return dot(columns[...], jnp.concatenate([b_hi, b_hi, b_lo], axis=0))

    group_sums(0, products(field[0, :, :, 8:32, :]))
    pl.semaphore_wait(barrier, greeted)
    send_sums(0)

    @pl.when(i_moved == 1)
    def _():
        send_factor().start()

    copies = send_halos(0)
    started = list(copies)
    fill_diagonal()
    fill_columns()
    fill_overlap()
    for k in range(DEGREE):
        send_atoms(k, copies)
        stencil(k, copies)
        scale_local(k)
        if k < DEGREE - 1:
            ready = products(local[...])
        rep = picked_rows(k)
        if k < DEGREE - 1:
            group_sums(k + 1, ready + projected(rep))
            send_sums(k + 1)
        returned = nonlocal_part(rep).reshape(ZI, XI, CY, 128)
        for zi in range(ZI):
            for xi in range(XI):
                value = local[zi, xi] + returned[zi, xi]
                if k < DEGREE - 1:
                    field[k + 1, zi, xi, 8:32, :] = value
                else:
                    for q in range(4):
                        zb, xb = q // 2, q % 2
                        out_ref[zb * ZI + zi, xb * XI + xi] = value[:, 32 * q : 32 * q + 32]
        if k < DEGREE - 1:
            copies = send_halos(k + 1)
            started += copies

    for copy in started:
        copy.wait_send()
    for k in range(DEGREE):
        sent = grouped.at[k, pl.ds(0, BESIDE)]
        pltpu.make_async_copy(sent, sent, sum_send.at[k, 0]).wait()

        @pl.when(i_moved == 0)
        def _():
            pltpu.make_async_copy(sent, sent, spread_send.at[k, 0]).wait()

        @pl.when(i_moved == 1)
        def _():
            own_sums(k).wait_send()

        @pl.when(hosting == 1)
        def _():
            whole = grouped.at[k]
            pltpu.make_async_copy(whole, whole, spread_send.at[k, 1]).wait()

    @pl.when(i_moved == 1)
    def _():
        send_factor().wait_send()


def shards(sizes, orbitals, potential, projectors, targets, coupling):
    cells = orbitals.transpose(1, 2, 3, 0)
    hbm = pl.BlockSpec(memory_space=pl.ANY)
    vmem = pl.BlockSpec(memory_space=pltpu.VMEM)
    steps = DEGREE
    result = pl.pallas_call(
        functools.partial(kernel, sizes),
        out_shape=jax.ShapeDtypeStruct((CZ, CX, CY, NORB), F32),
        in_specs=[hbm] * 5,
        out_specs=vmem,
        scratch_shapes=[
            pltpu.VMEM((CZ, CX, CY, NORB), F32),
            pltpu.VMEM((PROWS, CZ * CX * CY), F32),
            pltpu.VMEM((CZ * CX, CY), F32),
            pltpu.SMEM((SLOTS,), jnp.int32),
            pltpu.SMEM((ATOM_DEV * NPJ,), F32),
            pltpu.VMEM((steps, ZI, XI, CY + 16, 128), F32),
            pltpu.VMEM((steps, ZI, XI, CY, 128), F32),
            pltpu.VMEM((steps, ZI, XI, CY, 128), F32),
            pltpu.VMEM((steps, ZI, 2, CY, 128), F32),
            pltpu.VMEM((steps, ZI, 2, CY, 128), F32),
            pltpu.VMEM((steps, ZI, CY, 128), F32),
            pltpu.VMEM((steps, ZI, CY, 128), F32),
            pltpu.VMEM((steps, ZI, CY, 128), F32),
            pltpu.VMEM((steps, ZI, CY, 128), F32),
            pltpu.VMEM((steps, BESIDE + 1, 8, 128), F32),
            pltpu.VMEM((steps, 2 * BESIDE + 1, 8, 128), F32),
            pltpu.VMEM((steps, 2, 8, 128), F32),
            pltpu.VMEM((steps, 32, 8, 128), F32),
            pltpu.VMEM((4 * PROWS, 384), F32),
            pltpu.VMEM((4 * PROWS, 384), BF16),
            pltpu.VMEM((4 * PROWS, 384), BF16),
            pltpu.VMEM((ROWS, 768), BF16),
            pltpu.VMEM((8 * (BESIDE + 1), 128), F32),
            pltpu.VMEM((PROWS, 256), BF16),
            pltpu.VMEM((2, PROWS, PROWS), BF16),
            pltpu.VMEM((8, 128), F32),
            pltpu.VMEM((8, 128), F32),
            pltpu.VMEM((ZI, XI, CY, 128), F32),
            pltpu.VMEM((128, 128), F32),
            pltpu.VMEM((ZI, XI, CY, 128), F32),
            pltpu.SemaphoreType.DMA((5,)),
            pltpu.SemaphoreType.DMA((steps, 8)),
            pltpu.SemaphoreType.DMA((steps, 8)),
            pltpu.SemaphoreType.DMA((steps, 2)),
            pltpu.SemaphoreType.DMA((steps, 2)),
            pltpu.SemaphoreType.DMA((steps, 2)),
            pltpu.SemaphoreType.DMA((steps, 2)),
            pltpu.SemaphoreType.DMA((2,)),
        ],
        compiler_params=pltpu.CompilerParams(
            collective_id=0, has_side_effects=True, vmem_limit_bytes=60 * 1024 * 1024
        ),
    )(
        cells,
        potential.reshape(CZ * CX, CY),
        projectors.reshape(PROWS, CZ * CX * CY),
        targets.reshape(SLOTS),
        coupling.reshape(ATOM_DEV * NPJ),
    )
    return result.transpose(3, 0, 1, 2)


def solution(mesh):
    sizes = {name: mesh.shape[name] for name in ("gx", "gy", "gz")}
    return jax.shard_map(
        functools.partial(shards, sizes),
        mesh=mesh,
        in_specs=(
            P(None, "gz", "gx", "gy"),
            P("gz", "gx", "gy"),
            P("gz", "gx", "gy", None, None),
            P("gz", "gx", "gy", None),
            P("gz", "gx", "gy", None),
        ),
        out_specs=P(None, "gz", "gx", "gy"),
        check_vma=False,
    )
```

```python
import functools

import jax
import jax.numpy as jnp
from jax import lax
from jax.experimental import pallas as pl
from jax.experimental.pallas import tpu as pltpu
from jax.sharding import PartitionSpec as P

MESH = pl.DeviceIdType.MESH
F32, BF16 = jnp.float32, jnp.bfloat16

DEGREE = 3
NORB, NPJ, SLOTS, ATOM_DEV = 32, 4, 16, 8
CZ, CX, CY = 6, 8, 24
PROWS = SLOTS * NPJ
ZI, XI = CZ // 2, CX // 2
ROWS = ZI * XI * CY
SEG_CELLS = XI * CY

STENCIL = (
    -5369.0 / 1800.0,
    12.0 / 7.0,
    -15.0 / 56.0,
    10.0 / 189.0,
    -1.0 / 112.0,
    2.0 / 1925.0,
    -1.0 / 16632.0,
)
LOWER_EDGE = 2.0
UPPER_EDGE = 16.0
CENTRE = 0.5 * (UPPER_EDGE + LOWER_EDGE)
SPREAD = 0.5 * (UPPER_EDGE - LOWER_EDGE)
WEIGHT = tuple(-0.5 * c / SPREAD for c in STENCIL)

OFFSETS = [
    (a - 1, b - 1, c - 1)
    for a in range(3)
    for b in range(3)
    for c in range(3)
    if (a, b, c) != (1, 1, 1)
]
BESIDE = len(OFFSETS)
RUN = 8


def pick_place(gz, gx, runs, inverse):
    run, y, core = gz // RUN, lax.rem(gz, RUN), lax.rem(gx, 2)
    last = runs - 1
    step = -1 if inverse else 1
    at_end, at_start = y == RUN - 1, y == 0
    upper, lower = core == 1, core == 0
    low, high = run == 0, run == last
    if inverse:
        shift_up, shift_down = at_end & upper & ~low, at_start & lower & ~high
        wrap_up, wrap_down = at_end & lower & low, at_start & upper & high
    else:
        shift_up, shift_down = at_end & upper & ~high, at_start & lower & ~low
        wrap_up, wrap_down = at_end & lower & high, at_start & upper & low
    moved = jnp.where(shift_up | wrap_down, 1, 0) + jnp.where(shift_down | wrap_up, 1, 0)
    runs_on = jnp.where(shift_up, step, jnp.where(shift_down, -step, 0))
    runs_on = jnp.where(wrap_up, -step * last, jnp.where(wrap_down, step * last, runs_on))
    return gz + RUN * runs_on, moved


def split2(value):
    high = value.astype(BF16)
    low = (value - high.astype(F32)).astype(BF16)
    return high, low


def split3(value):
    high = value.astype(BF16)
    rest = value - high.astype(F32)
    mid = rest.astype(BF16)
    low = (rest - mid.astype(F32)).astype(BF16)
    return high, mid, low


def in_pairs(values):
    while len(values) > 1:
        paired = [a + b for a, b in zip(values[::2], values[1::2])]
        values = paired + values[len(paired) * 2 :]
    return values[0]


def dot(a, b):
    return jnp.dot(a, b, preferred_element_type=F32)


def lanes_of(shape):
    return lax.broadcasted_iota(jnp.int32, shape, len(shape) - 1)


def roll(value, shift):
    return pltpu.roll(value, shift, value.ndim - 1)


def kernel(
    sizes,
    orb_hbm,
    pot_hbm,
    proj_hbm,
    targets_hbm,
    coupling_hbm,
    out_ref,
    orb,
    proj,
    pot_ref,
    targets_ref,
    coupling_ref,
    field,
    z_low,
    z_high,
    x_low,
    x_high,
    x_low_part,
    x_high_part,
    send_low_part,
    send_high_part,
    grouped,
    partials,
    scaled,
    gathered,
    rows_t,
    rows_hi,
    rows_lo,
    columns,
    choose,
    choose_half,
    pick,
    overlap,
    factor,
    guest_factor,
    diagonal,
    pot_pad,
    local,
    in_sems,
    halo_send,
    halo_recv,
    sum_send,
    sum_recv,
    spread_send,
    spread_recv,
    factor_sems,
):
    me = {name: lax.axis_index(name) for name in ("gz", "gx", "gy")}

    def beside(offset):
        place = {
            name: lax.rem(me[name] + step + sizes[name], sizes[name])
            for name, step in zip(("gz", "gx", "gy"), offset)
        }
        return (place["gx"], place["gy"], place["gz"])

    runs = sizes["gz"] // RUN

    def host_of(place):
        gz, moved = pick_place(place[2], place[0], runs, False)
        return (place[0], place[1], gz), moved

    targets = [beside(offset) for offset in OFFSETS]
    hosts = [host_of(place) for place in targets]
    my_host, i_moved = host_of((me["gx"], me["gy"], me["gz"]))
    guest_gz, hosting = pick_place(me["gz"], me["gx"], runs, True)
    guest = (me["gx"], me["gy"], guest_gz)
    around_guest = [
        tuple(
            lax.rem(at + step + sizes[name], sizes[name])
            for name, at, step in zip(("gx", "gy", "gz"), guest, (offset[1], offset[2], offset[0]))
        )
        for offset in OFFSETS
    ]

    barrier = pltpu.get_barrier_semaphore()

    def greet(place):
        pl.semaphore_signal(barrier, inc=1, device_id=place, device_id_type=MESH)

    greeted = 27 * hosting + i_moved
    for offset, place, (host, moved) in zip(OFFSETS, targets, hosts):
        direct = 1 if sum(map(abs, offset)) == 1 else 1 - i_moved * moved
        greeted = greeted + moved + direct
        if isinstance(direct, int):
            greet(place)
        else:
            pl.when(direct == 1)(functools.partial(greet, place))
        pl.when(moved == 1)(functools.partial(greet, host))
    pl.when(i_moved == 1)(functools.partial(greet, my_host))

    @pl.when(hosting == 1)
    def _():
        greet(guest)
        for place in around_guest:
            greet(place)

    loads = [
        pltpu.make_async_copy(source, target, in_sems.at[i])
        for i, (source, target) in enumerate(
            (
                (orb_hbm, orb),
                (proj_hbm, proj),
                (targets_hbm, targets_ref),
                (coupling_hbm, coupling_ref),
                (pot_hbm, pot_ref),
            )
        )
    ]
    for load in loads:
        load.start()

    loads[0].wait()
    for zi in range(ZI):
        for xi in range(XI):
            for q in range(4):
                zb, xb = q // 2, q % 2
                field[0, zi, xi, 8:32, 32 * q : 32 * q + 32] = orb[zb * ZI + zi, xb * XI + xi]

    loads[1].wait()
    for q in range(4):
        zb, xb = q // 2, q % 2
        for zi in range(ZI):
            start = (zb * ZI + zi) * CX * CY + xb * SEG_CELLS
            rows_t[PROWS * q : PROWS * (q + 1), SEG_CELLS * zi : SEG_CELLS * (zi + 1)] = proj[
                :, start : start + SEG_CELLS
            ]
    rows_t[:, ROWS:384] = jnp.zeros((4 * PROWS, 384 - ROWS), F32)
    high, low = split2(rows_t[...])
    rows_hi[...] = high
    rows_lo[...] = low

    loads[2].wait()
    loads[3].wait()
    lane_slot = lanes_of((8, 128)) % PROWS // NPJ
    row_slot = lax.broadcasted_iota(jnp.int32, (PROWS, 256), 0) // NPJ
    named_lane = jnp.zeros((8, 128), jnp.int32)
    named_row = jnp.zeros((PROWS, 256), jnp.int32)
    own_first = ATOM_DEV * (BESIDE // 2)
    for s in range(SLOTS):
        atom = targets_ref[s]
        atom = jnp.where(
            atom < own_first,
            atom,
            jnp.where(atom < own_first + ATOM_DEV, atom + own_first, atom - ATOM_DEV),
        )
        named_lane = jnp.where(lane_slot == s, atom, named_lane)
        named_row = jnp.where(row_slot == s, atom, named_row)
    atom_row = lax.broadcasted_iota(jnp.int32, (8, 128), 0)
    for j in range(BESIDE + 1):
        choose[8 * j : 8 * j + 8, :] = jnp.where(named_lane == atom_row + 8 * j, 1.0, 0.0)
    choose[8 * (BESIDE + 1) :, :] = jnp.zeros((8, 128), F32)
    choose_half[...] = choose[...].astype(BF16)
    pick[...] = jnp.where(named_row == lanes_of((PROWS, 256)), 1.0, 0.0).astype(BF16)
    for k in range(DEGREE):
        for j in range(BESIDE + 1, 32):
            gathered[k, j] = jnp.zeros((8, 128), F32)
    pair = NPJ * lax.broadcasted_iota(jnp.int32, (8, 128), 0) + lanes_of((8, 128)) // NORB
    weights = jnp.zeros((8, 128), F32)
    for j in range(ATOM_DEV * NPJ):
        weights = jnp.where(pair == j, coupling_ref[j], weights)
    factor[...] = weights * (1.0 / SPREAD)

    group = lanes_of((PROWS, 128)) // NORB
    own_group = group == lax.broadcasted_iota(jnp.int32, (PROWS, 128), 0) % NPJ
    is_x1 = lanes_of((CY, 128)) % 64 >= 32
    is_z1 = lanes_of((CY, 128)) >= 64

    def everywhere(masked):
        paired = masked + roll(masked, 64)
        return paired + roll(paired, 32)

    def products(cells):
        f_hi, f_lo = split2(cells.reshape(ROWS, 128))
        p_hi, p_lo = rows_hi[:, :ROWS], rows_lo[:, :ROWS]
        crossed = dot(p_hi, f_hi) + (dot(p_lo, f_hi) + dot(p_hi, f_lo))
        kept = crossed[3 * PROWS :]
        for q in range(3):
            kept = jnp.where(group == q, crossed[PROWS * q : PROWS * (q + 1)], kept)
        return everywhere(kept)

    def group_sums(k, by_row):
        stacked = jnp.concatenate(split2(jnp.where(own_group, by_row, 0.0)), axis=0)
        sums = dot(choose_half[...], stacked)
        grouped[k] = sums[: 8 * (BESIDE + 1)].reshape(BESIDE + 1, 8, 128)

    def send_sums(k):
        for j, (place, moved) in enumerate(hosts):
            pltpu.make_async_remote_copy(
                src_ref=grouped.at[k, j],
                dst_ref=partials.at[k, j + BESIDE * moved],
                send_sem=sum_send.at[k, 0],
                recv_sem=sum_recv.at[k, moved],
                device_id=place,
                device_id_type=MESH,
            ).start()

        @pl.when(i_moved == 1)
        def _():
            own_sums(k).start()

    def own_sums(k):
        return pltpu.make_async_remote_copy(
            src_ref=grouped.at[k, BESIDE],
            dst_ref=partials.at[k, 2 * BESIDE],
            send_sem=sum_send.at[k, 1],
            recv_sem=sum_recv.at[k, 1],
            device_id=my_host,
            device_id_type=MESH,
        )

    def send_factor():
        return pltpu.make_async_remote_copy(
            src_ref=factor,
            dst_ref=guest_factor,
            send_sem=factor_sems.at[0],
            recv_sem=factor_sems.at[1],
            device_id=my_host,
            device_id_type=MESH,
        )

    def halo_copies(k):
        own = field.at[k, :, :, pl.ds(8, CY), :]
        moves = (
            (own, z_low.at[k], (1, 0, 0)),
            (own, z_high.at[k], (-1, 0, 0)),
            (field.at[k, :, :, pl.ds(24, 8), :], field.at[k, :, :, pl.ds(0, 8), :], (0, 0, 1)),
            (field.at[k, :, :, pl.ds(8, 8), :], field.at[k, :, :, pl.ds(32, 8), :], (0, 0, -1)),
            (field.at[k, :, pl.ds(2, 2), pl.ds(8, CY), :], x_low.at[k], (0, 1, 0)),
            (field.at[k, :, pl.ds(0, 2), pl.ds(8, CY), :], x_high.at[k], (0, -1, 0)),
            (send_low_part.at[k], x_low_part.at[k], (0, 1, 0)),
            (send_high_part.at[k], x_high_part.at[k], (0, -1, 0)),
        )
        return [
            pltpu.make_async_remote_copy(
                src_ref=source,
                dst_ref=target,
                send_sem=halo_send.at[k, i],
                recv_sem=halo_recv.at[k, i],
                device_id=beside(offset),
                device_id_type=MESH,
            )
            for i, (source, target, offset) in enumerate(moves)
        ]

    def send_halos(k):
        for zi in range(ZI):
            cell = [field[k, zi, xi, 8:32, :] for xi in range(XI)]
            send_low_part[k, zi] = jnp.where(is_x1, cell[1], roll(cell[0], 96))
            send_high_part[k, zi] = jnp.where(is_x1, roll(cell[2], 32), cell[3])
        copies = halo_copies(k)
        for copy in copies[2:]:
            copy.start()
        return copies

    def fill_overlap():
        o_hi, o_lo = split2(proj[...])

        def rows_by_rows(a, b):
            return lax.dot_general(a, b, (((1,), (1,)), ((), ())), preferred_element_type=F32)

        gram = rows_by_rows(o_hi, o_hi) + (rows_by_rows(o_hi, o_lo) + rows_by_rows(o_lo, o_hi))
        g_hi, g_lo = split2(gram)
        overlap[0] = g_hi
        overlap[1] = g_lo

    loads[4].wait()
    pot_pad[...] = jnp.zeros((128, 128), F32)
    pot_pad[: CZ * CX, :CY] = pot_ref[...]
    pot_t = pot_pad[...].T[:CY]
    pieces = split3(pot_t)
    stacked_pot = jnp.concatenate([p.astype(F32) for p in pieces], axis=0).astype(BF16)
    plane = lax.broadcasted_iota(jnp.int32, (128, 128), 0)
    lane = lanes_of((128, 128))
    wanted = (lane // 64 * ZI) * CX + lane // 32 % 2 * XI

    def fill_diagonal():
        for zi in range(ZI):
            for xi in range(XI):
                hot = jnp.where(plane == wanted + (zi * CX + xi), 1.0, 0.0).astype(BF16)
                got = dot(stacked_pot, hot)
                value = got[:CY] + (got[CY : 2 * CY] + got[2 * CY :])
                diagonal[zi, xi] = (value - (CENTRE + 1.5 * STENCIL[0])) * (1.0 / SPREAD)

    def fill_columns():
        transposed = rows_t[...].T[:ROWS]
        t_hi, t_lo = split2(transposed)
        columns[:, 0:256] = t_hi
        columns[:, 256:512] = t_lo
        columns[:, 512:768] = t_hi

    def spread(k, which, place, slot):
        return pltpu.make_async_remote_copy(
            src_ref=scaled.at[k, which],
            dst_ref=gathered.at[k, slot],
            send_sem=spread_send.at[k, which],
            recv_sem=spread_recv.at[k, 0 if slot < BESIDE else 1],
            device_id=place,
            device_id_type=MESH,
        )

    def send_atoms(k, copies):
        for behind, copy in zip(copies[2:4], copies[:2]):
            behind.wait_recv()
            copy.start()
        @pl.when(i_moved == 0)
        def _():
            landed = partials.at[k, pl.ds(0, BESIDE)]
            pltpu.make_async_copy(landed, landed, sum_recv.at[k, 0]).wait()
            total = in_pairs([grouped[k, BESIDE]] + [partials[k, j] for j in range(BESIDE)])
            total = total * factor[...]
            scaled[k, 0] = total
            for j, place in enumerate(targets):
                spread(k, 0, place, BESIDE - 1 - j).start()
            gathered[k, BESIDE] = total

        @pl.when(hosting == 1)
        def _():
            landed = partials.at[k, pl.ds(BESIDE, BESIDE + 1)]
            pltpu.make_async_copy(landed, landed, sum_recv.at[k, 1]).wait()
            if k == 0:
                send_factor().wait_recv()
            total = in_pairs([partials[k, j] for j in range(BESIDE, 2 * BESIDE + 1)])
            scaled[k, 1] = total * guest_factor[...]
            for j, place in enumerate(around_guest):
                spread(k, 1, place, BESIDE - 1 - j).start()
            spread(k, 1, guest, BESIDE).start()

    def stencil(k, copies):
        for copy in copies[:2] + copies[4:]:
            copy.wait_recv()
        for xi in range(XI):
            own = [field[k, zi, xi, 8:32, :] for zi in range(ZI)]
            low = [z_low[k, zi, xi] for zi in range(ZI)]
            high = [z_high[k, zi, xi] for zi in range(ZI)]
            before = [roll(jnp.where(is_z1, l, o), 64) for o, l in zip(own, low)]
            after = [roll(jnp.where(is_z1, o, h), 64) for o, h in zip(own, high)]
            line = low + before + own + after + high
            for zi in range(ZI):
                at = zi + 2 * ZI
                total = diagonal[zi, xi] * own[zi]
                for d in range(1, 7):
                    total = total + WEIGHT[d] * (line[at - d] + line[at + d])
                for d in range(1, 7):
                    total = total + WEIGHT[d] * (
                        field[k, zi, xi, 8 - d : 32 - d, :] + field[k, zi, xi, 8 + d : 32 + d, :]
                    )
                local[zi, xi] = total
        for zi in range(ZI):
            own = [field[k, zi, xi, 8:32, :] for xi in range(XI)]
            up = [roll(o, 32) for o in own]
            down = [roll(o, 96) for o in own]
            low = [x_low[k, zi, i] for i in range(2)]
            high = [x_high[k, zi, i] for i in range(2)]
            low_part, high_part = x_low_part[k, zi], x_high_part[k, zi]
            before = [
                jnp.where(is_x1, up[0], low_part),
                jnp.where(is_x1, up[1], roll(low_part, 96)),
                jnp.where(is_x1, up[2], roll(low[0], 96)),
                jnp.where(is_x1, up[3], roll(low[1], 96)),
            ]
            after = [
                jnp.where(is_x1, roll(high[0], 32), down[0]),
                jnp.where(is_x1, roll(high[1], 32), down[1]),
                jnp.where(is_x1, high_part, down[2]),
                jnp.where(is_x1, roll(high_part, 32), down[3]),
            ]
            line = low + before + own + after + high
            for xi in range(XI):
                at = xi + 6
                total = local[zi, xi]
                for d in range(1, 7):
                    total = total + WEIGHT[d] * (line[at - d] + line[at + d])
                local[zi, xi] = total

    def scale_local(k):
        if k > 0:
            for zi in range(ZI):
                for xi in range(XI):
                    local[zi, xi] = 2.0 * local[zi, xi] - field[k - 1, zi, xi, 8:32, :]

    def picked_rows(k):
        landed = gathered.at[k, pl.ds(0, BESIDE)]
        pltpu.make_async_copy(landed, landed, spread_recv.at[k, 0]).wait()

        @pl.when(i_moved == 1)
        def _():
            own = gathered.at[k, BESIDE]
            pltpu.make_async_copy(own, own, spread_recv.at[k, 1]).wait()

        a, b = split2(gathered[k].reshape(256, 128))
        hot = pick[...]
        picked = dot(hot, a) + dot(hot, b)
        rep = everywhere(jnp.where(own_group, picked, 0.0))
        return rep if k == 0 else 2.0 * rep

    def projected(rep):
        r_hi, r_lo = split2(rep)
        return dot(overlap[0], r_hi) + (dot(overlap[1], r_hi) + dot(overlap[0], r_lo))

    def nonlocal_part(rep):
        blocks = jnp.concatenate([jnp.where(group == q, rep, 0.0) for q in range(4)], axis=0)
        b_hi, b_lo = split2(blocks)
        return dot(columns[...], jnp.concatenate([b_hi, b_hi, b_lo], axis=0))

    group_sums(0, products(field[0, :, :, 8:32, :]))
    pl.semaphore_wait(barrier, greeted)
    send_sums(0)

    @pl.when(i_moved == 1)
    def _():
        send_factor().start()

    copies = send_halos(0)
    started = list(copies)
    fill_diagonal()
    fill_columns()
    fill_overlap()
    for k in range(DEGREE):
        send_atoms(k, copies)
        stencil(k, copies)
        scale_local(k)
        if k < DEGREE - 1:
            ready = products(local[...])
        rep = picked_rows(k)
        if k < DEGREE - 1:
            group_sums(k + 1, ready + projected(rep))
            send_sums(k + 1)
        returned = nonlocal_part(rep).reshape(ZI, XI, CY, 128)
        for zi in range(ZI):
            for xi in range(XI):
                value = local[zi, xi] + returned[zi, xi]
                if k < DEGREE - 1:
                    field[k + 1, zi, xi, 8:32, :] = value
                else:
                    for q in range(4):
                        zb, xb = q // 2, q % 2
                        out_ref[zb * ZI + zi, xb * XI + xi] = value[:, 32 * q : 32 * q + 32]
        if k < DEGREE - 1:
            copies = send_halos(k + 1)
            started += copies

    for copy in started:
        copy.wait_send()
    for k in range(DEGREE):
        sent = grouped.at[k, pl.ds(0, BESIDE)]
        pltpu.make_async_copy(sent, sent, sum_send.at[k, 0]).wait()

        @pl.when(i_moved == 0)
        def _():
            pltpu.make_async_copy(sent, sent, spread_send.at[k, 0]).wait()

        @pl.when(i_moved == 1)
        def _():
            own_sums(k).wait_send()

        @pl.when(hosting == 1)
        def _():
            whole = grouped.at[k]
            pltpu.make_async_copy(whole, whole, spread_send.at[k, 1]).wait()

    @pl.when(i_moved == 1)
    def _():
        send_factor().wait_send()


def shards(sizes, orbitals, potential, projectors, targets, coupling):
    cells = orbitals.transpose(1, 2, 3, 0)
    hbm = pl.BlockSpec(memory_space=pl.ANY)
    vmem = pl.BlockSpec(memory_space=pltpu.VMEM)
    steps = DEGREE
    result = pl.pallas_call(
        functools.partial(kernel, sizes),
        out_shape=jax.ShapeDtypeStruct((CZ, CX, CY, NORB), F32),
        in_specs=[hbm] * 5,
        out_specs=vmem,
        scratch_shapes=[
            pltpu.VMEM((CZ, CX, CY, NORB), F32),
            pltpu.VMEM((PROWS, CZ * CX * CY), F32),
            pltpu.VMEM((CZ * CX, CY), F32),
            pltpu.SMEM((SLOTS,), jnp.int32),
            pltpu.SMEM((ATOM_DEV * NPJ,), F32),
            pltpu.VMEM((steps, ZI, XI, CY + 16, 128), F32),
            pltpu.VMEM((steps, ZI, XI, CY, 128), F32),
            pltpu.VMEM((steps, ZI, XI, CY, 128), F32),
            pltpu.VMEM((steps, ZI, 2, CY, 128), F32),
            pltpu.VMEM((steps, ZI, 2, CY, 128), F32),
            pltpu.VMEM((steps, ZI, CY, 128), F32),
            pltpu.VMEM((steps, ZI, CY, 128), F32),
            pltpu.VMEM((steps, ZI, CY, 128), F32),
            pltpu.VMEM((steps, ZI, CY, 128), F32),
            pltpu.VMEM((steps, BESIDE + 1, 8, 128), F32),
            pltpu.VMEM((steps, 2 * BESIDE + 1, 8, 128), F32),
            pltpu.VMEM((steps, 2, 8, 128), F32),
            pltpu.VMEM((steps, 32, 8, 128), F32),
            pltpu.VMEM((4 * PROWS, 384), F32),
            pltpu.VMEM((4 * PROWS, 384), BF16),
            pltpu.VMEM((4 * PROWS, 384), BF16),
            pltpu.VMEM((ROWS, 768), BF16),
            pltpu.VMEM((8 * (BESIDE + 2), 128), F32),
            pltpu.VMEM((8 * (BESIDE + 2), 128), BF16),
            pltpu.VMEM((PROWS, 256), BF16),
            pltpu.VMEM((2, PROWS, PROWS), BF16),
            pltpu.VMEM((8, 128), F32),
            pltpu.VMEM((8, 128), F32),
            pltpu.VMEM((ZI, XI, CY, 128), F32),
            pltpu.VMEM((128, 128), F32),
            pltpu.VMEM((ZI, XI, CY, 128), F32),
            pltpu.SemaphoreType.DMA((5,)),
            pltpu.SemaphoreType.DMA((steps, 8)),
            pltpu.SemaphoreType.DMA((steps, 8)),
            pltpu.SemaphoreType.DMA((steps, 2)),
            pltpu.SemaphoreType.DMA((steps, 2)),
            pltpu.SemaphoreType.DMA((steps, 2)),
            pltpu.SemaphoreType.DMA((steps, 2)),
            pltpu.SemaphoreType.DMA((2,)),
        ],
        compiler_params=pltpu.CompilerParams(
            collective_id=0, has_side_effects=True, vmem_limit_bytes=60 * 1024 * 1024
        ),
    )(
        cells,
        potential.reshape(CZ * CX, CY),
        projectors.reshape(PROWS, CZ * CX * CY),
        targets.reshape(SLOTS),
        coupling.reshape(ATOM_DEV * NPJ),
    )
    return result.transpose(3, 0, 1, 2)


def solution(mesh):
    sizes = {name: mesh.shape[name] for name in ("gx", "gy", "gz")}
    return jax.shard_map(
        functools.partial(shards, sizes),
        mesh=mesh,
        in_specs=(
            P(None, "gz", "gx", "gy"),
            P("gz", "gx", "gy"),
            P("gz", "gx", "gy", None, None),
            P("gz", "gx", "gy", None),
            P("gz", "gx", "gy", None),
        ),
        out_specs=P(None, "gz", "gx", "gy"),
        check_vma=False,
    )
```
